256 devices in a mesh: dp: 16 (over z, core), ctx: 16 (over x, y).
Axes of the slice: x: 4, y: 4, z: 8, core: 2. Of those that a mesh axis runs over, the one named last changes fastest.
Arguments:
- ssm_input: bfloat16 [16, 4096, 5120], P('dp', 'ctx'), may hold values from -6 to 6
- gate_input: bfloat16 [16, 4096, 5120], P('dp', 'ctx'), may hold values from -6 to 6
- input_map: bfloat16 [16, 4096, 128], P('dp', 'ctx'), may hold values from -6 to 6
- output_map: bfloat16 [16, 4096, 128], P('dp', 'ctx'), may hold values from -6 to 6
- step_size: float32 [16, 80, 4096], P('dp', None, 'ctx'), may hold values from 0.00024414062 to 1.2009766
- log_rate: float32 [80], replicated
- entry_state: bfloat16 [16, 16, 80, 64, 128], P('dp', 'ctx'), may hold values from -0.59765625 to 0.59765625
- norm_gain: float32 [5120], replicated, may hold values from 0.18 to 5.5
- out_weight: bfloat16 [5120, 1280], P(('dp', 'ctx')), may hold values from -0.078125 to 0.078125
- out_grad: bfloat16 [16, 4096, 1280], P('dp', 'ctx')
Outputs:
- input_grad: bfloat16 [16, 4096, 5120], P('dp', 'ctx')
- clipped_grad: float32 [5120, 1280], P('ctx', 'dp')
The draws below stay inside these ranges and needn't reach their ends.
All inputs are finite; a program needn't handle non-finite values.
Results may differ from the reference program's by a relative error of at most 0.014.
Values may be sent and summed in bfloat16 or wider, within the bound.
A program may use at most 192 MiB of HBM per device.

```python
import math
import jax
import jax.numpy as jnp
from jax import lax

D = 1280
HEADS = 80
HEAD_DIM = 64
STATE = 128
TOK = 256
IN = 5120
SEQ = 4096
EXAMPLES = 16
N_CTX = 16


def draw_step_size(key, part):
    key = jax.random.fold_in(key, 11)
    base_key, spot_key = jax.random.split(key)
    shape = (EXAMPLES, HEADS, SEQ)
    spots = jax.random.randint(spot_key, (EXAMPLES, 1, 1, 2), 0, SEQ)
    positions = jnp.arange(SEQ)[None, None, :, None]
    rough = jnp.exp(jax.random.uniform(base_key, shape, jnp.float32, -0.6931, 0.6931))
    hits = jnp.max((positions == spots).astype(jnp.float32), axis=-1)
    return 2.0 / SEQ * rough + 1.2 * hits


def draw_log_rate(key, part):
    key = jax.random.fold_in(key, 12)
    pick_key, slow_key, fast_key = jax.random.split(key, 3)
    share = 0.5
    fast = jax.random.uniform(pick_key, (HEADS,), jnp.float32) < share
    slow_value = jax.random.uniform(slow_key, (HEADS,), jnp.float32, -1.609, -0.693)
    upper = jnp.log(jnp.float32(SEQ) / 80.0) + 0.47
    lower = jnp.maximum(upper - 2.9, -1.6)
    fast_value = lower + (upper - lower) * jax.random.uniform(fast_key, (HEADS,), jnp.float32)
    return jnp.where(fast, fast_value, slow_value)


def draw_norm_gain(key, part):
    key = jax.random.fold_in(key, 13)
    slope = 0.275
    trend = jnp.exp(slope * (2.0 * jnp.arange(IN, dtype=jnp.float32) / IN - 1.0))
    rough = jnp.exp(jax.random.uniform(key, (IN,), jnp.float32, -1.15, 1.15))
    return trend * rough


def draw_out_grad(key, part):
    key = jax.random.fold_in(key, 14)
    noise_key, column_key = jax.random.split(key, 2)
    shape = (EXAMPLES, SEQ, D)
    columns = jnp.exp(jax.random.uniform(column_key, (D,), jnp.float32, -1.15, 1.15))
    noise = jax.random.normal(noise_key, shape, jnp.float32)
    return (noise * columns).astype(jnp.bfloat16)


def shard_levels(own_key, shape, pieces, least, high):
    gain, own = 1.0, jax.random.fold_in(own_key, 6)
    for axis_at, parts in pieces:
        heights = jnp.exp(jax.random.uniform(jax.random.fold_in(own, axis_at), (parts,), jnp.float32, least / len(pieces), high / len(pieces)))
        gain = gain * jnp.repeat(heights, shape[axis_at] // parts).reshape([-1 if axis == axis_at else 1 for axis in range(len(shape))])
    return gain


def scatter_about(own_key, dims, scale, bound, cuts=(), kind=jnp.bfloat16):
    gain = shard_levels(own_key, dims, cuts, -0.22, 0.18) if cuts else 1.0
    drawn = jax.random.normal(own_key, dims, jnp.float32) * scale * gain
    return jnp.minimum(jnp.maximum(drawn, -bound), bound).astype(kind)


def setup_inputs(seed: int = 0) -> dict:
    keys = jax.random.split(jax.random.key(seed), 11)
    return {
        "ssm_input": scatter_about(keys[0], (EXAMPLES, SEQ, IN), 1.0, 6.0, ((0, 16), (1, 16))),
        "gate_input": scatter_about(keys[1], (EXAMPLES, SEQ, IN), 1.0, 6.0, ((0, 16), (1, 16))),
        "input_map": scatter_about(keys[2], (EXAMPLES, SEQ, STATE), 1.0, 6.0, ((0, 16), (1, 16))),
        "output_map": scatter_about(keys[3], (EXAMPLES, SEQ, STATE), 1.0, 6.0, ((0, 16), (1, 16))),
        "step_size": draw_step_size(jax.random.fold_in(keys[10], 71), 0),
        "log_rate": draw_log_rate(jax.random.fold_in(keys[10], 71), 0),
        "entry_state": scatter_about(keys[6], (EXAMPLES, N_CTX, HEADS, HEAD_DIM, STATE), 0.1, 0.59765625, ((0, 16), (1, 16))),
        "norm_gain": draw_norm_gain(jax.random.fold_in(keys[10], 71), 0),
        "out_weight": scatter_about(keys[8], (IN, D), IN ** -0.5, 0.078125, ((0, 256),)),
        "out_grad": draw_out_grad(jax.random.fold_in(keys[10], 71), 0),
    }


NORM_EPS = 1e-05
CLIP_EPS = 1e-06

def head_block(scaled, cumulative, coupling, c_full, b_full, start_state):
    length = cumulative.shape[-1]
    log_gap = cumulative[:, :, :, None] - cumulative[:, :, None, :]
    causal = jnp.arange(length)[:, None] >= jnp.arange(length)[None, :]
    decay_map = jnp.exp(jnp.where(causal, log_gap, -1e+30))
    mixing = decay_map * coupling[:, None, :, :]
    inside = jnp.einsum('egtu,eugp->etgp', mixing, scaled)
    carried = jnp.einsum('etn,egpn->etgp', c_full, start_state)
    carried = carried * jnp.exp(cumulative).transpose(0, 2, 1)[:, :, :, None]
    final_log = cumulative[:, :, -1:]
    tail_decay = jnp.exp(final_log - cumulative)
    end_state = jnp.exp(final_log)[:, :, :, None] * start_state
    end_state = end_state + jnp.einsum('egu,eugp,eun->egpn', tail_decay, scaled, b_full)
    return (inside + carried, end_state)

def scan_forward(values, step, rate_vec, b_full, c_full, start_state):
    blocks, length, inner_dim = values.shape
    head_count = rate_vec.shape[0]
    head_size = inner_dim // head_count
    group_size = math.gcd(head_count, 8)
    group_count = head_count // group_size
    cumulative = jnp.cumsum(-step * rate_vec[None, :, None], axis=-1)
    scaled = values.reshape(blocks, length, head_count, head_size) * step.transpose(0, 2, 1)[:, :, :, None]
    coupling = jnp.einsum('etn,eun->etu', c_full, b_full)
    scaled_groups = scaled.reshape(blocks, length, group_count, group_size, head_size).transpose(2, 0, 1, 3, 4)
    cumul_groups = cumulative.reshape(blocks, group_count, group_size, length).transpose(1, 0, 2, 3)
    state_groups = start_state.reshape(blocks, group_count, group_size, head_size, -1).transpose(1, 0, 2, 3, 4)

    def per_block(operands):
        return head_block(operands[0], operands[1], coupling, c_full, b_full, operands[2])
    outputs, finals = lax.map(per_block, (scaled_groups, cumul_groups, state_groups))
    y_value = outputs.transpose(1, 2, 0, 3, 4).reshape(blocks, length, inner_dim)
    end_state = finals.transpose(1, 0, 2, 3, 4).reshape(blocks, head_count, head_size, -1)
    return (y_value, end_state)

def gated_norm(values, gate_f, norm_gain):
    mixed = values * jax.nn.silu(gate_f)
    inverse_rms = lax.rsqrt(lax.optimization_barrier(jnp.mean(mixed * mixed, axis=-1, keepdims=True)) + NORM_EPS)
    return mixed * inverse_rms * norm_gain

def chain_terms(y_grad, step, rate_vec, c_full):
    blocks, length, inner_dim = y_grad.shape
    head_count = rate_vec.shape[0]
    cumulative = jnp.cumsum(-step * rate_vec[None, :, None], axis=-1)
    weighted = y_grad.reshape(blocks, length, head_count, -1) * jnp.exp(cumulative).transpose(0, 2, 1)[:, :, :, None]
    pushed = jnp.einsum('ethp,etn->ehpn', weighted, c_full)
    return (jnp.exp(cumulative[:, :, -1]), pushed)

def reference(ssm_input, gate_input, input_map, output_map, step_size, log_rate, entry_state, norm_gain, out_weight, out_grad):
    rate_vec = jnp.exp(log_rate)
    inner_dim = ssm_input.shape[-1]

    def per_example(total, operands):
        x_ex, z_ex, b_ex, c_ex, step_ex, state_ex, dout_ex = operands
        values = x_ex.reshape(N_CTX, TOK, inner_dim).astype(jnp.float32)
        b_full = b_ex.reshape(N_CTX, TOK, -1).astype(jnp.float32)
        c_full = c_ex.reshape(N_CTX, TOK, -1).astype(jnp.float32)
        gate_f = z_ex.reshape(N_CTX, TOK, inner_dim).astype(jnp.float32)
        step_blocks = step_ex.reshape(HEADS, N_CTX, TOK).transpose(1, 0, 2)
        start_state = state_ex.astype(jnp.float32)
        dout_blocks = dout_ex.reshape(N_CTX, TOK, D)

        def forward(inputs_f):
            return scan_forward(inputs_f, step_blocks, rate_vec, b_full, c_full, start_state)
        (y_value, end_state), pullback = jax.vjp(forward, values)

        def normalize(inputs_y):
            return gated_norm(inputs_y, gate_f, norm_gain)
        normed, norm_pull = jax.vjp(normalize, y_value)
        gated = normed.astype(jnp.bfloat16)
        gated_grad = jnp.dot(dout_ex, out_weight.T, preferred_element_type=jnp.float32)
        y_grad, = norm_pull(gated_grad.reshape(N_CTX, TOK, inner_dim))
        factors, pushed = chain_terms(y_grad, step_blocks, rate_vec, c_full)

        def backstep(carry, terms):
            factor_k, pushed_k = terms
            return (factor_k[:, None, None] * carry + pushed_k, carry)
        zero_state = jnp.zeros(pushed.shape[1:], jnp.float32)
        _, state_grad = lax.scan(backstep, zero_state, (factors, pushed), reverse=True)
        input_f, = pullback((y_grad, state_grad))

        def add_block(accum, pair):
            gated_blk, dout_blk = pair
            term = jnp.dot(gated_blk.T, dout_blk, preferred_element_type=jnp.float32)
            return (accum + term, None)
        weight_grad, _ = lax.scan(add_block, jnp.zeros((inner_dim, D), jnp.float32), (gated, dout_blocks))
        clip = jnp.minimum(1.0, lax.rsqrt(jnp.sum(weight_grad * weight_grad) + CLIP_EPS))
        return (total + clip * weight_grad, input_f.reshape(SEQ, inner_dim).astype(jnp.bfloat16))
    start_total = jnp.zeros((inner_dim, D), jnp.float32)
    total, input_grad = lax.scan(per_example, start_total, (ssm_input, gate_input, input_map, output_map, step_size, entry_state, out_grad))
    clipped_grad = total * math.sqrt(IN * D / EXAMPLES)
    return (input_grad, clipped_grad)
```

```python
import functools
import math

import jax
import jax.numpy as jnp
from jax import lax
from jax.experimental import pallas as pl
from jax.experimental.pallas import tpu as pltpu
from jax.sharding import PartitionSpec as P

NORM_EPS = 1e-05
CLIP_EPS = 1e-06
MESH = pl.DeviceIdType.MESH
F32 = jnp.float32
BF16 = jnp.bfloat16
HIGHEST = lax.Precision.HIGHEST

TOK = 256
HALF = 128
STATE = 128
GROUP = 8
LANES = 512
GROUPS = 10
INNER = 5120
MODEL = 1280
CAP = 80.0
SIDE = 4
CTX = 16
OWN = INNER // CTX
WIDE = 384
COLS = MODEL // 16
HALFIN = INNER // 2
VMEM_BYTES = 56 * 1024 * 1024


def params(**extra):
    return pltpu.CompilerParams(vmem_limit_bytes=VMEM_BYTES, **extra)


def dot(a, b):
    return jnp.dot(a, b, preferred_element_type=F32)


def dot_nt(a, b):
    return lax.dot_general(a, b, (((1,), (1,)), ((), ())), preferred_element_type=F32)


def dot_tn(a, b):
    return lax.dot_general(a, b, (((0,), (0,)), ((), ())), preferred_element_type=F32)


def rows_of(shape):
    return lax.broadcasted_iota(jnp.int32, shape, 0)


def lanes_of(shape):
    return lax.broadcasted_iota(jnp.int32, shape, 1)


def decay_rows(step, log_rate, upper):
    drop = -(jnp.exp(log_rate) * step)
    cumulative = jnp.dot(drop, upper, preferred_element_type=F32, precision=HIGHEST)
    return cumulative, cumulative - jnp.log(step)


def upper_ones():
    shape = (TOK, TOK)
    return jnp.where(rows_of(shape) <= lanes_of(shape), 1.0, 0.0).astype(F32)


def pair_cols(columns, pair):
    low = lanes_of((TOK, HALF)) < HALF // 2
    return jnp.where(low, columns[:, 2 * pair : 2 * pair + 1], columns[:, 2 * pair + 1 : 2 * pair + 2])


def silu(gate):
    return gate / (1.0 + jnp.exp(-gate))


def forward_kernel(
    x_ref, z_ref, st_ref, lr_ref, s_ref, b_ref, c_ref, gain_ref, gated_ref, r_ref, mixed, coup, upper, acc
):
    at = pl.program_id(0)

    @pl.when(at == 0)
    def _():
        shape = (TOK, TOK)
        both = dot_nt(c_ref[...], b_ref[...])
        coup[...] = jnp.where(rows_of(shape) >= lanes_of(shape), both, 0.0)
        upper[...] = upper_ones()
        acc[...] = jnp.zeros_like(acc)

    cumulative, shifted = decay_rows(st_ref[...], lr_ref[...], upper[...])
    columns = cumulative.T
    low = lanes_of((TOK, HALF)) < HALF // 2
    for pair in range(GROUP // 2):
        lanes = slice(pair * HALF, (pair + 1) * HALF)
        x_pair = x_ref[:, lanes]
        zero = jnp.zeros_like(x_pair)
        parts = (jnp.where(low, x_pair, zero), jnp.where(low, zero, x_pair))
        top = bottom = None
        for which in range(2):
            head = 2 * pair + which
            col = columns[:, head : head + 1]
            row = shifted[head : head + 1, :]
            m_top = jnp.exp(jnp.minimum(col[:HALF] - row[:, :HALF], CAP)) * coup[:HALF, :HALF]
            m_bot = jnp.exp(jnp.minimum(col[HALF:] - row, CAP)) * coup[HALF:, :]
            t = dot(m_top.astype(BF16), parts[which][:HALF])
            b = dot(m_bot.astype(BF16), parts[which])
            top = t if top is None else top + t
            bottom = b if bottom is None else bottom + b
        inside = jnp.concatenate([top, bottom], axis=0)
        carried = dot_nt(c_ref[...], s_ref[lanes, :])
        y = inside + carried * jnp.exp(pair_cols(columns, pair))
        mix = y * silu(z_ref[:, lanes].astype(F32))
        mixed[at, :, lanes] = mix
        acc[...] += mix * mix

    @pl.when(at == GROUPS - 1)
    def _():
        mean = jnp.sum(acc[...], axis=1, keepdims=True) * (1.0 / INNER)
        r = lax.rsqrt(mean + NORM_EPS)
        r_ref[...] = jnp.broadcast_to(r, r_ref.shape)
        for g in range(GROUPS):
            lanes = slice(g * LANES, (g + 1) * LANES)
            gated_ref[:, lanes] = (mixed[g] * r * gain_ref[:, lanes]).astype(BF16)


def forward(x, z, step, log_rate, state, b, c, gain):
    block = lambda i: (0, i)
    whole = lambda i: (0, 0)
    return pl.pallas_call(
        forward_kernel,
        grid=(GROUPS,),
        out_shape=(jax.ShapeDtypeStruct((TOK, INNER), BF16), jax.ShapeDtypeStruct((TOK, HALF), F32)),
        in_specs=[
            pl.BlockSpec((TOK, LANES), block),
            pl.BlockSpec((TOK, LANES), block),
            pl.BlockSpec((GROUP, TOK), lambda i: (i, 0)),
            pl.BlockSpec((GROUP, 1), lambda i: (i, 0)),
            pl.BlockSpec((LANES, STATE), lambda i: (i, 0)),
            pl.BlockSpec((TOK, STATE), whole),
            pl.BlockSpec((TOK, STATE), whole),
            pl.BlockSpec((1, INNER), whole),
        ],
        out_specs=(pl.BlockSpec((TOK, INNER), whole), pl.BlockSpec((TOK, HALF), whole)),
        scratch_shapes=[
            pltpu.VMEM((GROUPS, TOK, LANES), F32),
            pltpu.VMEM((TOK, TOK), F32),
            pltpu.VMEM((TOK, TOK), F32),
            pltpu.VMEM((TOK, HALF), F32),
        ],
        compiler_params=params(),
        cost_estimate=pl.CostEstimate(flops=3 * 10**9, bytes_accessed=10 * 10**6, transcendentals=10**7),
        name="scan_forward",
    )(x, z, step, log_rate, state, b, c, gain)


def norm_kernel(
    og_ref, w_ref, gated_ref, z_ref, r_ref, gain_ref, st_ref, lr_ref, c_ref, yg_ref, push_ref, gg, acc, upper, ct
):
    phase, at = pl.program_id(0), pl.program_id(1)

    @pl.when(jnp.logical_and(phase == 0, at == 0))
    def _():
        acc[...] = jnp.zeros_like(acc)
        upper[...] = upper_ones()
        ct[...] = c_ref[...].astype(F32).T.astype(BF16)

    @pl.when(phase == 0)
    def _():
        value = dot_nt(og_ref[...], w_ref[...])
        gg[at] = value
        product = value * gated_ref[...].astype(F32)
        total = acc[...]
        for i in range(LANES // HALF):
            total += product[:, i * HALF : (i + 1) * HALF]
        acc[...] = total

    @pl.when(phase == 1)
    def _():
        @pl.when(at == 0)
        def _():
            mean = jnp.sum(acc[...], axis=1, keepdims=True) * (1.0 / INNER)
            acc[...] = jnp.broadcast_to(mean, acc.shape)

        cumulative, _ = decay_rows(st_ref[...], lr_ref[...], upper[...])
        columns = cumulative.T
        for pair in range(GROUP // 2):
            lanes = slice(pair * HALF, (pair + 1) * HALF)
            gain = gain_ref[:, lanes]
            inner = gain * gg[at, :, lanes] - gated_ref[:, lanes].astype(F32) * (1.0 / gain) * acc[...]
            yg = silu(z_ref[:, lanes].astype(F32)) * r_ref[...] * inner
            yg_ref[:, lanes] = yg.astype(BF16)
            weighted = (yg * jnp.exp(pair_cols(columns, pair))).astype(BF16)
            push_ref[:, lanes] = dot(ct[...], weighted).astype(BF16)


def norm_backward(og, w, gated, z, r, gain, step, log_rate, c):
    whole = lambda p, i: (0, 0)
    lane = lambda p, i: (0, i)
    late = lambda p, i: (0, i * p)
    late_rows = lambda p, i: (i * p, 0)
    return pl.pallas_call(
        norm_kernel,
        grid=(2, GROUPS),
        out_shape=(jax.ShapeDtypeStruct((TOK, INNER), BF16), jax.ShapeDtypeStruct((STATE, INNER), BF16)),
        in_specs=[
            pl.BlockSpec((TOK, MODEL), whole),
            pl.BlockSpec((LANES, MODEL), lambda p, i: (jnp.where(p == 0, i, GROUPS - 1), 0)),
            pl.BlockSpec((TOK, LANES), lane),
            pl.BlockSpec((TOK, LANES), late),
            pl.BlockSpec((TOK, HALF), whole),
            pl.BlockSpec((1, LANES), late),
            pl.BlockSpec((GROUP, TOK), late_rows),
            pl.BlockSpec((GROUP, 1), late_rows),
            pl.BlockSpec((TOK, STATE), whole),
        ],
        out_specs=(pl.BlockSpec((TOK, LANES), late), pl.BlockSpec((STATE, LANES), late)),
        scratch_shapes=[
            pltpu.VMEM((GROUPS, TOK, LANES), F32),
            pltpu.VMEM((TOK, HALF), F32),
            pltpu.VMEM((TOK, TOK), F32),
            pltpu.VMEM((STATE, TOK), BF16),
        ],
        compiler_params=params(),
        cost_estimate=pl.CostEstimate(flops=4 * 10**9, bytes_accessed=25 * 10**6, transcendentals=3 * 10**6),
        name="norm_backward",
    )(og, w, gated, z, r, gain, step, log_rate, c)


def backward_kernel(yg_ref, sg_ref, st_ref, lr_ref, b_ref, c_ref, out_ref, coup, upper):
    at = pl.program_id(0)

    @pl.when(at == 0)
    def _():
        shape = (TOK, TOK)
        both = dot_nt(b_ref[...], c_ref[...])
        coup[...] = jnp.where(rows_of(shape) <= lanes_of(shape), both, 0.0)
        upper[...] = upper_ones()

    cumulative, shifted = decay_rows(st_ref[...], lr_ref[...], upper[...])
    columns = shifted.T
    last = (cumulative[:, TOK - 1 :] - shifted).T
    low = lanes_of((TOK, HALF)) < HALF // 2
    for pair in range(GROUP // 2):
        lanes = slice(pair * HALF, (pair + 1) * HALF)
        yg = yg_ref[:, lanes]
        zero = jnp.zeros_like(yg)
        parts = (jnp.where(low, yg, zero), jnp.where(low, zero, yg))
        top = bottom = None
        for which in range(2):
            head = 2 * pair + which
            col = columns[:, head : head + 1]
            row = cumulative[head : head + 1, :]
            m_top = jnp.exp(jnp.minimum(row - col[:HALF], CAP)) * coup[:HALF, :]
            m_bot = jnp.exp(jnp.minimum(row[:, HALF:] - col[HALF:], CAP)) * coup[HALF:, HALF:]
            t = dot(m_top.astype(BF16), parts[which])
            b = dot(m_bot.astype(BF16), parts[which][HALF:])
            top = t if top is None else top + t
            bottom = b if bottom is None else bottom + b
        inside = jnp.concatenate([top, bottom], axis=0)
        ended = dot(b_ref[...], sg_ref[:, lanes])
        out_ref[:, lanes] = (inside + ended * jnp.exp(pair_cols(last, pair))).astype(BF16)


def scan_backward(yg, sg, step, log_rate, b, c):
    block = lambda i: (0, i)
    whole = lambda i: (0, 0)
    return pl.pallas_call(
        backward_kernel,
        grid=(GROUPS,),
        out_shape=jax.ShapeDtypeStruct((TOK, INNER), BF16),
        in_specs=[
            pl.BlockSpec((TOK, LANES), block),
            pl.BlockSpec((STATE, LANES), block),
            pl.BlockSpec((GROUP, TOK), lambda i: (i, 0)),
            pl.BlockSpec((GROUP, 1), lambda i: (i, 0)),
            pl.BlockSpec((TOK, STATE), whole),
            pl.BlockSpec((TOK, STATE), whole),
        ],
        out_specs=pl.BlockSpec((TOK, LANES), block),
        scratch_shapes=[pltpu.VMEM((TOK, TOK), F32), pltpu.VMEM((TOK, TOK), F32)],
        compiler_params=params(),
        cost_estimate=pl.CostEstimate(flops=3 * 10**9, bytes_accessed=8 * 10**6, transcendentals=10**7),
        name="scan_backward",
    )(yg, sg, step, log_rate, b, c)


def weight_kernel(*refs):
    gs, os, out_ref = refs[:SIDE], refs[SIDE : 2 * SIDE], refs[2 * SIDE]
    for chunk in range(SIDE):
        total = None
        for g, o in zip(gs, os):
            part = dot_tn(g[:, chunk * OWN : (chunk + 1) * OWN], o[...])
            total = part if total is None else total + part
        out_ref[chunk] = total.astype(BF16)


def weight_partials(gs, os):
    return pl.pallas_call(
        weight_kernel,
        out_shape=jax.ShapeDtypeStruct((SIDE, OWN, MODEL), BF16),
        compiler_params=params(),
        cost_estimate=pl.CostEstimate(flops=4 * 10**9, bytes_accessed=9 * 10**6, transcendentals=0),
        name="weight_partials",
    )(*gs, *os)


def exchange_kernel(
    scale,
    push_ref,
    fac_ref,
    t0_ref,
    t1_ref,
    t2_ref,
    t3_ref,
    sg_ref,
    out_ref,
    arrived,
    facs,
    running,
    spread,
    back,
    landed,
    squares,
    square_own,
    turned,
    chunks,
    paired,
    zsend,
    zrecv,
    p_send,
    p_recv,
    f_send,
    f_recv,
    b_send,
    b_recv,
    q_send,
    q_recv,
    pair_send,
    pair_recv,
    z_send,
    z_recv,
):
    dp, me = lax.axis_index("dp"), lax.axis_index("ctx")
    core, z = lax.rem(dp, 2), lax.div(dp, 2)
    partner = dp + 1 - 2 * core

    barrier = pltpu.get_barrier_semaphore()

    def greet(s, carry):
        pl.semaphore_signal(barrier, inc=1, device_id=(dp, lax.rem(me + s, CTX)), device_id_type=MESH)
        return carry

    def greet_z(s, carry):
        other = 2 * lax.rem(z + s, 8) + core
        pl.semaphore_signal(barrier, inc=1, device_id=(other, me), device_id_type=MESH)
        return carry

    lax.fori_loop(1, CTX, greet, 0)
    lax.fori_loop(1, 8, greet_z, 0)
    pl.semaphore_signal(barrier, inc=1, device_id=(partner, me), device_id_type=MESH)
    pl.semaphore_wait(barrier, CTX - 1 + 7 + 1)

    def piece(ref, owner):
        row = pl.multiple_of(lax.div(owner, 2) * 16, 16)
        lane = pl.multiple_of(lax.rem(owner, 2) * HALFIN, HALFIN)
        return ref.at[pl.ds(row, 16), pl.ds(lane, HALFIN)]

    def push_copy(src, to, slot):
        return pltpu.make_async_remote_copy(
            src_ref=piece(push_ref, src),
            dst_ref=arrived.at[slot],
            send_sem=p_send.at[to],
            recv_sem=p_recv.at[slot],
            device_id=(dp, to),
            device_id_type=MESH,
        )

    def fac_copy(to, slot):
        return pltpu.make_async_remote_copy(
            src_ref=fac_ref,
            dst_ref=facs.at[slot],
            send_sem=f_send.at[to],
            recv_sem=f_recv.at[slot],
            device_id=(dp, to),
            device_id_type=MESH,
        )

    def back_copy(to, owner):
        return pltpu.make_async_remote_copy(
            src_ref=back.at[to],
            dst_ref=piece(landed, owner),
            send_sem=b_send.at[to],
            recv_sem=b_recv.at[owner],
            device_id=(dp, to),
            device_id_type=MESH,
        )

    def square_copy(to, slot):
        return pltpu.make_async_remote_copy(
            src_ref=square_own,
            dst_ref=squares.at[slot],
            send_sem=q_send.at[to],
            recv_sem=q_recv.at[slot],
            device_id=(dp, to),
            device_id_type=MESH,
        )

    pair_copy = pltpu.make_async_remote_copy(
        src_ref=chunks.at[1 - core],
        dst_ref=paired,
        send_sem=pair_send,
        recv_sem=pair_recv,
        device_id=(partner, me),
        device_id_type=MESH,
    )

    def z_copy(to, slot):
        return pltpu.make_async_remote_copy(
            src_ref=zsend.at[to],
            dst_ref=zrecv.at[slot],
            send_sem=z_send.at[to],
            recv_sem=z_recv.at[slot],
            device_id=(2 * to + core, me),
            device_id_type=MESH,
        )

    def others(body):
        def turn(s, carry):
            body(lax.rem(me + s, CTX))
            return carry

        lax.fori_loop(1, CTX, turn, 0)

    def send_pushed(to):
        fac_copy(to, me).start()
        push_copy(to, to, me).start()

    others(send_pushed)

    total = t0_ref[...].astype(F32) + t1_ref[...].astype(F32) + t2_ref[...].astype(F32) + t3_ref[...].astype(F32)
    turned[...] = jnp.zeros_like(turned)
    turned[:OWN, :] = total
    square_own[...] = jnp.sum(jnp.sum((total * total).reshape(OWN // 8, 8, MODEL), axis=0).reshape(8, 10, 128), axis=1)
    others(lambda to: square_copy(to, me).start())

    arrived[me] = piece(push_ref, me)[...]
    facs[me] = fac_ref[...]
    others(lambda k: fac_copy(k, k).wait_recv())
    shape = (HALF, HALFIN)
    head = lax.shift_right_logical(lanes_of(shape) + lax.rem(me, 2) * HALFIN, 6)
    hot = jnp.where(rows_of(shape) == head, 1.0, 0.0).astype(F32)
    listed = jnp.concatenate([facs[k][:1, :] for k in range(CTX)], axis=0)
    wide = jnp.dot(listed, hot, preferred_element_type=F32, precision=HIGHEST)
    for k in range(CTX):
        spread[k] = jnp.broadcast_to(wide[k : k + 1], (8, HALFIN))
    running[...] = jnp.zeros_like(running)

    def chain(turn, carry):
        k = CTX - 1 - turn

        @pl.when(k != me)
        def _():
            push_copy(k, k, k).wait_recv()

        now = running[...]
        back[k] = now.astype(BF16)

        @pl.when(k != me)
        def _():
            back_copy(k, me).start()

        factor = spread[k]
        running[...] = jnp.concatenate([factor, factor], axis=0) * now + arrived[k].astype(F32)
        return carry

    lax.fori_loop(0, CTX, chain, 0)
    piece(landed, me)[...] = back[me]

    others(lambda k: square_copy(k, k).wait_recv())
    squares[me] = square_own[...]
    all_squares = squares[0]
    for k in range(1, CTX):
        all_squares += squares[k]
    whole = jnp.sum(jnp.sum(all_squares, axis=1, keepdims=True), axis=0, keepdims=True)
    clip = jnp.minimum(1.0, lax.rsqrt(whole + CLIP_EPS)) * scale
    for i in range(MODEL // HALF):
        block = (turned[:, i * HALF : (i + 1) * HALF] * clip).T
        lo = i * HALF
        while lo < (i + 1) * HALF:
            owner = lo // COLS
            hi = min((i + 1) * HALF, (owner + 1) * COLS)
            at = slice(lo - owner * COLS, hi - owner * COLS)
            chunks[owner % 2, owner // 2, at] = block[lo - i * HALF : hi - i * HALF].astype(BF16)
            lo = hi
    pair_copy.start()
    pair_copy.wait_recv()

    def add_pair(i, carry):
        zsend[i] = (chunks[core, i].astype(F32) + paired[i].astype(F32)).astype(BF16)
        return carry

    lax.fori_loop(0, 8, add_pair, 0)

    def z_others(body):
        def turn(s, carry):
            body(lax.rem(z + s, 8))
            return carry

        lax.fori_loop(1, 8, turn, 0)

    z_others(lambda to: z_copy(to, z).start())
    others(lambda k: back_copy(me, k).wait_recv())
    sg_ref[...] = landed[...]
    z_others(lambda k: z_copy(k, k).wait_recv())
    zrecv[z] = zsend[z]
    summed = zrecv[0].astype(F32)
    for k in range(1, 8):
        summed += zrecv[k].astype(F32)
    padded = jnp.concatenate([summed, jnp.zeros((HALF - COLS, WIDE), F32)], axis=0).T
    out_ref[...] = padded[:OWN, :COLS]

    def finish(to):
        fac_copy(to, me).wait_send()
        push_copy(to, to, me).wait_send()
        square_copy(to, me).wait_send()
        back_copy(to, me).wait_send()

    others(finish)
    pair_copy.wait_send()
    z_others(lambda to: z_copy(to, z).wait_send())


def exchange(pushed, factors, terms, scale):
    vmem = pl.BlockSpec(memory_space=pltpu.VMEM)
    return pl.pallas_call(
        functools.partial(exchange_kernel, scale),
        out_shape=(jax.ShapeDtypeStruct((STATE, INNER), BF16), jax.ShapeDtypeStruct((OWN, COLS), F32)),
        in_specs=[vmem] * 6,
        out_specs=(vmem, vmem),
        scratch_shapes=[
            pltpu.VMEM((CTX, 16, HALFIN), BF16),
            pltpu.VMEM((CTX, 8, HALF), F32),
            pltpu.VMEM((16, HALFIN), F32),
            pltpu.VMEM((CTX, 8, HALFIN), F32),
            pltpu.VMEM((CTX, 16, HALFIN), BF16),
            pltpu.VMEM((STATE, INNER), BF16),
            pltpu.VMEM((CTX, 8, HALF), F32),
            pltpu.VMEM((8, HALF), F32),
            pltpu.VMEM((WIDE, MODEL), F32),
            pltpu.VMEM((2, 8, COLS, WIDE), BF16),
            pltpu.VMEM((8, COLS, WIDE), BF16),
            pltpu.VMEM((8, COLS, WIDE), BF16),
            pltpu.VMEM((8, COLS, WIDE), BF16),
        ]
        + [pltpu.SemaphoreType.DMA((CTX,))] * 8
        + [pltpu.SemaphoreType.DMA, pltpu.SemaphoreType.DMA]
        + [pltpu.SemaphoreType.DMA((8,))] * 2,
        compiler_params=params(collective_id=0, has_side_effects=True),
        cost_estimate=pl.CostEstimate(flops=10**8, bytes_accessed=50 * 10**6, transcendentals=0),
        name="exchange",
    )(pushed, factors, *terms)


def move(value, axis, step):
    def source(i):
        return (i // SIDE, i % SIDE)

    pairs = []
    for i in range(CTX):
        x, y = source(i)
        to = ((x + step) % SIDE) * SIDE + y if axis == 0 else x * SIDE + (y + step) % SIDE
        pairs.append((i, to))
    return lax.ppermute(value, "ctx", pairs)


def per_device(
    ssm_input,
    gate_input,
    input_map,
    output_map,
    step_size,
    log_rate,
    entry_state,
    norm_gain,
    out_weight,
    out_grad,
):
    examples = lax.axis_size("dp")
    me = lax.axis_index("ctx")
    x, y = me // SIDE, me % SIDE
    ssm, gate, og = ssm_input[0], gate_input[0], out_grad[0]
    b, c, step = input_map[0], output_map[0], step_size[0]
    rates = log_rate.reshape(-1, 1)
    state = entry_state.reshape(INNER, STATE)
    gain = norm_gain.reshape(1, INNER)

    weights = lax.all_gather(out_weight, ("dp", "ctx"), axis=0, tiled=True)
    grads = [og] + [move(og, 0, s) for s in range(1, SIDE)]

    gated, r = forward(ssm, gate, step, rates, state, b, c, gain)
    factor = jnp.exp(-jnp.exp(log_rate) * jnp.sum(step, axis=-1))
    factors = jnp.broadcast_to(jnp.pad(factor, (0, HALF - factor.shape[0]))[None], (8, HALF))

    def columns(s):
        return lax.dynamic_slice_in_dim(gated, lax.rem(x + s, SIDE) * MODEL, MODEL, axis=1)

    gates = [columns(0)] + [move(columns(s), 0, s) for s in range(1, SIDE)]
    partial = weight_partials(gates, grads)

    def chunk(s):
        return lax.dynamic_index_in_dim(partial, lax.rem(y + s, SIDE), axis=0, keepdims=False)

    terms = [chunk(0)] + [move(chunk(s), 1, s) for s in range(1, SIDE)]

    y_grad, pushed = norm_backward(og, weights, gated, gate, r, gain, step, rates, c)
    scale = math.sqrt(INNER * MODEL / examples)
    state_grad, summed = exchange(pushed, factors, terms, scale)
    input_grad = scan_backward(y_grad, state_grad, step, rates, b, c)
    return (input_grad[None], summed)


def solution(mesh):
    placed = (
        P("dp", "ctx", None),
        P("dp", "ctx", None),
        P("dp", "ctx", None),
        P("dp", "ctx", None),
        P("dp", None, "ctx"),
        P(),
        P("dp", "ctx", None, None, None),
        P(),
        P(("dp", "ctx"), None),
        P("dp", "ctx", None),
    )
    return jax.shard_map(
        per_device,
        mesh=mesh,
        in_specs=placed,
        out_specs=(P("dp", "ctx", None), P("ctx", "dp")),
        check_vma=False,
    )
```

```python
import functools
import math

import jax
import jax.numpy as jnp
from jax import lax
from jax.experimental import pallas as pl
from jax.experimental.pallas import tpu as pltpu
from jax.sharding import PartitionSpec as P

NORM_EPS = 1e-05
CLIP_EPS = 1e-06
MESH = pl.DeviceIdType.MESH
F32 = jnp.float32
BF16 = jnp.bfloat16
HIGHEST = lax.Precision.HIGHEST

TOK = 256
HALF = 128
STATE = 128
GROUP = 10
LANES = 640
GROUPS = 8
INNER = 5120
MODEL = 1280
CAP = 80.0
SIDE = 4
CTX = 16
OWN = INNER // CTX
WIDE = 384
COLS = MODEL // 16
HALFIN = INNER // 2
VMEM_BYTES = 56 * 1024 * 1024


def params(**extra):
    return pltpu.CompilerParams(vmem_limit_bytes=VMEM_BYTES, **extra)


def dot(a, b):
    return jnp.dot(a, b, preferred_element_type=F32)


def dot_nt(a, b):
    return lax.dot_general(a, b, (((1,), (1,)), ((), ())), preferred_element_type=F32)


def dot_tn(a, b):
    return lax.dot_general(a, b, (((0,), (0,)), ((), ())), preferred_element_type=F32)


def rows_of(shape):
    return lax.broadcasted_iota(jnp.int32, shape, 0)


def lanes_of(shape):
    return lax.broadcasted_iota(jnp.int32, shape, 1)


def decay_rows(step, log_rate, upper):
    drop = -(jnp.exp(log_rate) * step)
    cumulative = jnp.dot(drop, upper, preferred_element_type=F32, precision=HIGHEST)
    return cumulative, cumulative - jnp.log(step)


def upper_ones():
    shape = (TOK, TOK)
    return jnp.where(rows_of(shape) <= lanes_of(shape), 1.0, 0.0).astype(F32)


def pair_cols(columns, pair):
    low = lanes_of((TOK, HALF)) < HALF // 2
    return jnp.where(low, columns[:, 2 * pair : 2 * pair + 1], columns[:, 2 * pair + 1 : 2 * pair + 2])


def silu(gate):
    return gate / (1.0 + jnp.exp(-gate))


def gather_kernel(
    x_ref,
    z_ref,
    st_ref,
    lr_ref,
    s_ref,
    b_ref,
    c_ref,
    gain_ref,
    w_ref,
    og_ref,
    gated_ref,
    r_ref,
    gg_ref,
    mean_ref,
    gx_ref,
    ox_ref,
    mixed,
    coup,
    upper,
    acc,
    turned,
    thin,
    full,
    w_send,
    w_recv,
    ring_send,
    ring_recv,
    sib_send,
    sib_recv,
    o_send,
    o_recv,
    g_send,
    g_recv,
):
    dp, me = lax.axis_index("dp"), lax.axis_index("ctx")
    core, z = lax.rem(dp, 2), lax.div(dp, 2)
    x, y = lax.div(me, SIDE), lax.rem(me, SIDE)
    partner = dp + 1 - 2 * core

    barrier = pltpu.get_barrier_semaphore()

    def greet(s, carry):
        pl.semaphore_signal(barrier, inc=1, device_id=(dp, lax.rem(me + s, CTX)), device_id_type=MESH)
        return carry

    lax.fori_loop(1, CTX, greet, 0)
    for other in (2 * lax.rem(z + 1, 8) + core, 2 * lax.rem(z + 7, 8) + core, partner):
        pl.semaphore_signal(barrier, inc=1, device_id=(other, me), device_id_type=MESH)
    pl.semaphore_wait(barrier, CTX - 1 + 3)

    def thin_copy(to, slot):
        return pltpu.make_async_remote_copy(
            src_ref=w_ref,
            dst_ref=thin.at[slot],
            send_sem=w_send.at[to],
            recv_sem=w_recv.at[slot],
            device_id=(dp, to),
            device_id_type=MESH,
        )

    def half_block(at, which, half):
        row = pl.multiple_of(which * OWN + half * (OWN // 2), 16)
        return full.at[at, pl.ds(row, OWN // 2)]

    def ring_copy(way, turn, half, at):
        slot = (way * 4 + turn) * 2 + half
        step = 1 if way == 0 else 7
        return pltpu.make_async_remote_copy(
            src_ref=half_block(at, core, half),
            dst_ref=half_block(at, core, half),
            send_sem=ring_send.at[slot],
            recv_sem=ring_recv.at[slot],
            device_id=(2 * lax.rem(z + step, 8) + core, me),
            device_id_type=MESH,
        )

    def sib_copy(at, which, half):
        return pltpu.make_async_remote_copy(
            src_ref=half_block(at, which, half),
            dst_ref=half_block(at, which, half),
            send_sem=sib_send.at[at, half],
            recv_sem=sib_recv.at[at, half],
            device_id=(partner, me),
            device_id_type=MESH,
        )

    def o_copy(s, slot):
        return pltpu.make_async_remote_copy(
            src_ref=og_ref,
            dst_ref=ox_ref.at[slot],
            send_sem=o_send.at[s],
            recv_sem=o_recv.at[s],
            device_id=(dp, lax.rem(x + s, SIDE) * SIDE + y),
            device_id_type=MESH,
        )

    def g_copy(s, slot):
        to = lax.rem(x + s, SIDE)
        return pltpu.make_async_remote_copy(
            src_ref=turned.at[pl.ds(pl.multiple_of(to * MODEL, MODEL), MODEL)],
            dst_ref=gx_ref.at[slot],
            send_sem=g_send.at[s],
            recv_sem=g_recv.at[s],
            device_id=(dp, to * SIDE + y),
            device_id_type=MESH,
        )

    def others(body):
        def turn(s, carry):
            body(lax.rem(me + s, CTX))
            return carry

        lax.fori_loop(1, CTX, turn, 0)

    others(lambda to: thin_copy(to, me).start())
    for s in range(1, SIDE):
        o_copy(s, x).start()

    shape = (TOK, TOK)
    coup[...] = jnp.where(rows_of(shape) >= lanes_of(shape), dot_nt(c_ref[...], b_ref[...]), 0.0)
    upper[...] = upper_ones()
    acc[...] = jnp.zeros_like(acc)

    def group(at, carry):
        cumulative, shifted = decay_rows(st_ref[at], lr_ref[at], upper[...])
        columns = cumulative.T
        low = lanes_of((TOK, HALF)) < HALF // 2
        for pair in range(GROUP // 2):
            lanes = pl.ds(pl.multiple_of(at * LANES + pair * HALF, HALF), HALF)
            x_pair = x_ref[:, lanes]
            zero = jnp.zeros_like(x_pair)
            parts = (jnp.where(low, x_pair, zero), jnp.where(low, zero, x_pair))
            top = bottom = None
            for which in range(2):
                head = 2 * pair + which
                col = columns[:, head : head + 1]
                row = shifted[head : head + 1, :]
                m_top = jnp.exp(jnp.minimum(col[:HALF] - row[:, :HALF], CAP)) * coup[:HALF, :HALF]
                m_bot = jnp.exp(jnp.minimum(col[HALF:] - row, CAP)) * coup[HALF:, :]
                t = dot(m_top.astype(BF16), parts[which][:HALF])
                b = dot(m_bot.astype(BF16), parts[which])
                top = t if top is None else top + t
                bottom = b if bottom is None else bottom + b
            inside = jnp.concatenate([top, bottom], axis=0)
            carried = dot_nt(c_ref[...], s_ref[lanes, :])
            value = inside + carried * jnp.exp(pair_cols(columns, pair))
            mix = value * silu(z_ref[:, lanes].astype(F32))
            mixed[at, :, pair * HALF : (pair + 1) * HALF] = mix
            acc[...] += mix * mix
        return carry

    def arrive(turn, half):
        for way in (0, 1):
            if turn == 3 and half != way:
                continue
            at = lax.rem(z + (8 - turn - 1 if way == 0 else turn + 1), 8)
            ring_copy(way, turn, half, at).wait_recv()
            if turn < 2 or (turn == 2 and half == way):
                ring_copy(way, turn + 1, half, at).start()
            sib_copy(at, core, half).start()

    lax.fori_loop(0, 2, group, 0)

    thin[me] = w_ref[...]
    others(lambda k: thin_copy(k, k).wait_recv())
    rows = [thin[k][: OWN // CTX].astype(F32) for k in range(CTX)]
    own = pl.ds(pl.multiple_of(core * OWN, 16), OWN)
    full[z, own] = jnp.concatenate(rows, axis=0).astype(BF16)
    for half in range(2):
        for way in range(2):
            ring_copy(way, 0, half, z).start()
    for half in range(2):
        sib_copy(z, core, half).start()

    lax.fori_loop(2, 6, group, 0)
    arrive(0, 0)
    lax.fori_loop(6, GROUPS, group, 0)
    arrive(0, 1)

    r = lax.rsqrt(jnp.sum(acc[...], axis=1, keepdims=True) * (1.0 / INNER) + NORM_EPS)
    r_ref[...] = jnp.broadcast_to(r, r_ref.shape)

    def finish_norm(at, carry):
        lanes = pl.ds(pl.multiple_of(at * LANES, HALF), LANES)
        normed = mixed[at] * r_ref[:, :1] * gain_ref[:, lanes]
        gated_ref[:, lanes] = normed.astype(BF16)
        turned[lanes, :] = normed.T.astype(BF16)
        return carry

    lax.fori_loop(0, GROUPS, finish_norm, 0)
    for s in range(1, SIDE):
        g_copy(s, x).start()
    gx_ref[x] = turned[pl.ds(pl.multiple_of(x * MODEL, MODEL), MODEL), :]
    ox_ref[x] = og_ref[...]
    acc[...] = jnp.zeros_like(acc)

    def product(at):
        for half in range(2):
            sib_copy(at, 1 - core, half).wait_recv()
        value = dot_nt(og_ref[...], full[at])
        gg_ref[at] = value
        lanes = pl.ds(pl.multiple_of(at * LANES, HALF), LANES)
        both = value * gated_ref[:, lanes].astype(F32)
        total = acc[...]
        for i in range(LANES // HALF):
            total += both[:, i * HALF : (i + 1) * HALF]
        acc[...] = total

    arrive(1, 0)
    product(z)
    arrive(1, 1)
    product(lax.rem(z + 1, 8))
    arrive(2, 0)
    product(lax.rem(z + 7, 8))
    arrive(2, 1)
    product(lax.rem(z + 2, 8))
    arrive(3, 0)
    product(lax.rem(z + 6, 8))
    arrive(3, 1)
    product(lax.rem(z + 3, 8))
    product(lax.rem(z + 5, 8))
    product(lax.rem(z + 4, 8))
    mean = jnp.sum(acc[...], axis=1, keepdims=True) * (1.0 / INNER)
    mean_ref[...] = jnp.broadcast_to(mean, mean_ref.shape)

    for s in range(1, SIDE):
        source = lax.rem(x + SIDE - s, SIDE)
        o_copy(s, source).wait_recv()
        g_copy(s, source).wait_recv()
        o_copy(s, x).wait_send()
        g_copy(s, x).wait_send()
    others(lambda to: thin_copy(to, me).wait_send())
    for turn in range(4):
        for half in range(2):
            for way in range(2):
                if turn == 3 and half != way:
                    continue
                at = lax.rem(z + (8 - turn if way == 0 else turn), 8)
                ring_copy(way, turn, half, at).wait_send()

    def finish(at, carry):
        for half in range(2):
            sib_copy(at, core, half).wait_send()
        return carry

    lax.fori_loop(0, 8, finish, 0)


def gather(x, z, step, log_rate, state, b, c, gain, w, og):
    vmem = pl.BlockSpec(memory_space=pltpu.VMEM)
    dma = pltpu.SemaphoreType.DMA
    return pl.pallas_call(
        gather_kernel,
        out_shape=(
            jax.ShapeDtypeStruct((TOK, INNER), BF16),
            jax.ShapeDtypeStruct((TOK, HALF), F32),
            jax.ShapeDtypeStruct((GROUPS, TOK, LANES), F32),
            jax.ShapeDtypeStruct((TOK, HALF), F32),
            jax.ShapeDtypeStruct((SIDE, MODEL, TOK), BF16),
            jax.ShapeDtypeStruct((SIDE, TOK, MODEL), BF16),
        ),
        in_specs=[vmem] * 10,
        out_specs=(vmem,) * 6,
        scratch_shapes=[
            pltpu.VMEM((GROUPS, TOK, LANES), F32),
            pltpu.VMEM((TOK, TOK), F32),
            pltpu.VMEM((TOK, TOK), F32),
            pltpu.VMEM((TOK, HALF), F32),
            pltpu.VMEM((INNER, TOK), BF16),
            pltpu.VMEM((CTX, 32, MODEL), BF16),
            pltpu.VMEM((8, 2 * OWN, MODEL), BF16),
            dma((CTX,)),
            dma((CTX,)),
            dma((16,)),
            dma((16,)),
            dma((8, 2)),
            dma((8, 2)),
            dma((SIDE,)),
            dma((SIDE,)),
            dma((SIDE,)),
            dma((SIDE,)),
        ],
        compiler_params=params(collective_id=1, has_side_effects=True),
        cost_estimate=pl.CostEstimate(flops=7 * 10**9, bytes_accessed=60 * 10**6, transcendentals=10**7),
        name="gather",
    )(x, z, step, log_rate, state, b, c, gain, w, og)


def norm_kernel(gg_ref, gated_ref, z_ref, r_ref, mean_ref, gain_ref, st_ref, lr_ref, c_ref, yg_ref, push_ref, upper, ct):
    @pl.when(pl.program_id(0) == 0)
    def _():
        upper[...] = upper_ones()
        ct[...] = c_ref[...].astype(F32).T.astype(BF16)

    cumulative, _ = decay_rows(st_ref[0], lr_ref[0], upper[...])
    columns = cumulative.T
    for pair in range(GROUP // 2):
        lanes = slice(pair * HALF, (pair + 1) * HALF)
        gain = gain_ref[:, lanes]
        inner = gain * gg_ref[0, :, lanes] - gated_ref[:, lanes].astype(F32) * (1.0 / gain) * mean_ref[...]
        yg = silu(z_ref[:, lanes].astype(F32)) * r_ref[...] * inner
        yg_ref[:, lanes] = yg.astype(BF16)
        weighted = (yg * jnp.exp(pair_cols(columns, pair))).astype(BF16)
        push_ref[:, lanes] = dot(ct[...], weighted).astype(BF16)


def norm_backward(gg, gated, z, r, mean, gain, step, log_rate, c):
    whole = lambda i: (0, 0)
    lane = lambda i: (0, i)
    lead = lambda i: (i, 0, 0)
    return pl.pallas_call(
        norm_kernel,
        grid=(GROUPS,),
        out_shape=(jax.ShapeDtypeStruct((TOK, INNER), BF16), jax.ShapeDtypeStruct((STATE, INNER), BF16)),
        in_specs=[
            pl.BlockSpec((1, TOK, LANES), lead),
            pl.BlockSpec((TOK, LANES), lane),
            pl.BlockSpec((TOK, LANES), lane),
            pl.BlockSpec((TOK, HALF), whole),
            pl.BlockSpec((TOK, HALF), whole),
            pl.BlockSpec((1, LANES), lane),
            pl.BlockSpec((1, GROUP, TOK), lead),
            pl.BlockSpec((1, GROUP, 1), lead),
            pl.BlockSpec((TOK, STATE), whole),
        ],
        out_specs=(pl.BlockSpec((TOK, LANES), lane), pl.BlockSpec((STATE, LANES), lane)),
        scratch_shapes=[pltpu.VMEM((TOK, TOK), F32), pltpu.VMEM((STATE, TOK), BF16)],
        compiler_params=params(),
        cost_estimate=pl.CostEstimate(flops=10**9, bytes_accessed=15 * 10**6, transcendentals=3 * 10**6),
        name="norm_backward",
    )(gg, gated, z, r, mean, gain, step, log_rate, c)


def backward_kernel(yg_ref, sg_ref, st_ref, lr_ref, b_ref, c_ref, out_ref, coup, upper):
    at = pl.program_id(0)

    @pl.when(at == 0)
    def _():
        shape = (TOK, TOK)
        both = dot_nt(b_ref[...], c_ref[...])
        coup[...] = jnp.where(rows_of(shape) <= lanes_of(shape), both, 0.0)
        upper[...] = upper_ones()

    cumulative, shifted = decay_rows(st_ref[0], lr_ref[0], upper[...])
    columns = shifted.T
    last = (cumulative[:, TOK - 1 :] - shifted).T
    low = lanes_of((TOK, HALF)) < HALF // 2
    for pair in range(GROUP // 2):
        lanes = slice(pair * HALF, (pair + 1) * HALF)
        yg = yg_ref[:, lanes]
        zero = jnp.zeros_like(yg)
        parts = (jnp.where(low, yg, zero), jnp.where(low, zero, yg))
        top = bottom = None
        for which in range(2):
            head = 2 * pair + which
            col = columns[:, head : head + 1]
            row = cumulative[head : head + 1, :]
            m_top = jnp.exp(jnp.minimum(row - col[:HALF], CAP)) * coup[:HALF, :]
            m_bot = jnp.exp(jnp.minimum(row[:, HALF:] - col[HALF:], CAP)) * coup[HALF:, HALF:]
            t = dot(m_top.astype(BF16), parts[which])
            b = dot(m_bot.astype(BF16), parts[which][HALF:])
            top = t if top is None else top + t
            bottom = b if bottom is None else bottom + b
        inside = jnp.concatenate([top, bottom], axis=0)
        ended = dot(b_ref[...], sg_ref[:, lanes])
        out_ref[:, lanes] = (inside + ended * jnp.exp(pair_cols(last, pair))).astype(BF16)


def scan_backward(yg, sg, step, log_rate, b, c):
    block = lambda i: (0, i)
    whole = lambda i: (0, 0)
    return pl.pallas_call(
        backward_kernel,
        grid=(GROUPS,),
        out_shape=jax.ShapeDtypeStruct((TOK, INNER), BF16),
        in_specs=[
            pl.BlockSpec((TOK, LANES), block),
            pl.BlockSpec((STATE, LANES), block),
            pl.BlockSpec((1, GROUP, TOK), lambda i: (i, 0, 0)),
            pl.BlockSpec((1, GROUP, 1), lambda i: (i, 0, 0)),
            pl.BlockSpec((TOK, STATE), whole),
            pl.BlockSpec((TOK, STATE), whole),
        ],
        out_specs=pl.BlockSpec((TOK, LANES), block),
        scratch_shapes=[pltpu.VMEM((TOK, TOK), F32), pltpu.VMEM((TOK, TOK), F32)],
        compiler_params=params(),
        cost_estimate=pl.CostEstimate(flops=3 * 10**9, bytes_accessed=8 * 10**6, transcendentals=10**7),
        name="scan_backward",
    )(yg, sg, step, log_rate, b, c)


def weight_kernel(g_ref, o_ref, out_ref):
    for chunk in range(SIDE):
        total = None
        for source in range(SIDE):
            part = dot(g_ref[source, chunk * OWN : (chunk + 1) * OWN, :], o_ref[source])
            total = part if total is None else total + part
        out_ref[chunk] = total.astype(BF16)


def weight_partials(gs, os):
    return pl.pallas_call(
        weight_kernel,
        out_shape=jax.ShapeDtypeStruct((SIDE, OWN, MODEL), BF16),
        compiler_params=params(),
        cost_estimate=pl.CostEstimate(flops=4 * 10**9, bytes_accessed=9 * 10**6, transcendentals=0),
        name="weight_partials",
    )(gs, os)


def exchange_kernel(
    scale,
    push_ref,
    fac_ref,
    t0_ref,
    t1_ref,
    t2_ref,
    t3_ref,
    sg_ref,
    out_ref,
    arrived,
    facs,
    running,
    spread,
    back,
    landed,
    squares,
    square_own,
    turned,
    chunks,
    paired,
    zsend,
    zrecv,
    p_send,
    p_recv,
    f_send,
    f_recv,
    b_send,
    b_recv,
    q_send,
    q_recv,
    pair_send,
    pair_recv,
    z_send,
    z_recv,
):
    dp, me = lax.axis_index("dp"), lax.axis_index("ctx")
    core, z = lax.rem(dp, 2), lax.div(dp, 2)
    partner = dp + 1 - 2 * core

    barrier = pltpu.get_barrier_semaphore()

    def greet(s, carry):
        pl.semaphore_signal(barrier, inc=1, device_id=(dp, lax.rem(me + s, CTX)), device_id_type=MESH)
        return carry

    def greet_z(s, carry):
        other = 2 * lax.rem(z + s, 8) + core
        pl.semaphore_signal(barrier, inc=1, device_id=(other, me), device_id_type=MESH)
        return carry

    lax.fori_loop(1, CTX, greet, 0)
    lax.fori_loop(1, 8, greet_z, 0)
    pl.semaphore_signal(barrier, inc=1, device_id=(partner, me), device_id_type=MESH)
    pl.semaphore_wait(barrier, CTX - 1 + 7 + 1)

    def piece(ref, owner):
        row = pl.multiple_of(lax.div(owner, 2) * 16, 16)
        lane = pl.multiple_of(lax.rem(owner, 2) * HALFIN, HALFIN)
        return ref.at[pl.ds(row, 16), pl.ds(lane, HALFIN)]

    def push_copy(src, to, slot):
        return pltpu.make_async_remote_copy(
            src_ref=piece(push_ref, src),
            dst_ref=arrived.at[slot],
            send_sem=p_send.at[to],
            recv_sem=p_recv.at[slot],
            device_id=(dp, to),
            device_id_type=MESH,
        )

    def fac_copy(to, slot):
        return pltpu.make_async_remote_copy(
            src_ref=fac_ref,
            dst_ref=facs.at[slot],
            send_sem=f_send.at[to],
            recv_sem=f_recv.at[slot],
            device_id=(dp, to),
            device_id_type=MESH,
        )

    def back_copy(to, owner):
        return pltpu.make_async_remote_copy(
            src_ref=back.at[to],
            dst_ref=piece(landed, owner),
            send_sem=b_send.at[to],
            recv_sem=b_recv.at[owner],
            device_id=(dp, to),
            device_id_type=MESH,
        )

    def square_copy(to, slot):
        return pltpu.make_async_remote_copy(
            src_ref=square_own,
            dst_ref=squares.at[slot],
            send_sem=q_send.at[to],
            recv_sem=q_recv.at[slot],
            device_id=(dp, to),
            device_id_type=MESH,
        )

    pair_copy = pltpu.make_async_remote_copy(
        src_ref=chunks.at[1 - core],
        dst_ref=paired,
        send_sem=pair_send,
        recv_sem=pair_recv,
        device_id=(partner, me),
        device_id_type=MESH,
    )

    def z_copy(to, slot):
        return pltpu.make_async_remote_copy(
            src_ref=zsend.at[to],
            dst_ref=zrecv.at[slot],
            send_sem=z_send.at[to],
            recv_sem=z_recv.at[slot],
            device_id=(2 * to + core, me),
            device_id_type=MESH,
        )

    def others(body):
        def turn(s, carry):
            body(lax.rem(me + s, CTX))
            return carry

        lax.fori_loop(1, CTX, turn, 0)

    def send_pushed(to):
        fac_copy(to, me).start()
        push_copy(to, to, me).start()

    others(send_pushed)

    total = t0_ref[...].astype(F32) + t1_ref[...].astype(F32) + t2_ref[...].astype(F32) + t3_ref[...].astype(F32)
    turned[...] = jnp.zeros_like(turned)
    turned[:OWN, :] = total
    square_own[...] = jnp.sum(jnp.sum((total * total).reshape(OWN // 8, 8, MODEL), axis=0).reshape(8, 10, 128), axis=1)
    others(lambda to: square_copy(to, me).start())

    arrived[me] = piece(push_ref, me)[...]
    facs[me] = fac_ref[...]
    others(lambda k: fac_copy(k, k).wait_recv())
    shape = (HALF, HALFIN)
    head = lax.shift_right_logical(lanes_of(shape) + lax.rem(me, 2) * HALFIN, 6)
    hot = jnp.where(rows_of(shape) == head, 1.0, 0.0).astype(F32)
    listed = jnp.concatenate([facs[k][:1, :] for k in range(CTX)], axis=0)
    wide = jnp.dot(listed, hot, preferred_element_type=F32, precision=HIGHEST)
    for k in range(CTX):
        spread[k] = jnp.broadcast_to(wide[k : k + 1], (8, HALFIN))
    running[...] = jnp.zeros_like(running)

    def chain(turn, carry):
        k = CTX - 1 - turn

        @pl.when(k != me)
        def _():
            push_copy(k, k, k).wait_recv()

        now = running[...]
        back[k] = now.astype(BF16)

        @pl.when(k != me)
        def _():
            back_copy(k, me).start()

        factor = spread[k]
        running[...] = jnp.concatenate([factor, factor], axis=0) * now + arrived[k].astype(F32)
        return carry

    lax.fori_loop(0, CTX, chain, 0)
    piece(landed, me)[...] = back[me]

    others(lambda k: square_copy(k, k).wait_recv())
    squares[me] = square_own[...]
    all_squares = squares[0]
    for k in range(1, CTX):
        all_squares += squares[k]
    whole = jnp.sum(jnp.sum(all_squares, axis=1, keepdims=True), axis=0, keepdims=True)
    clip = jnp.minimum(1.0, lax.rsqrt(whole + CLIP_EPS)) * scale
    for i in range(MODEL // HALF):
        block = (turned[:, i * HALF : (i + 1) * HALF] * clip).T
        lo = i * HALF
        while lo < (i + 1) * HALF:
            owner = lo // COLS
            hi = min((i + 1) * HALF, (owner + 1) * COLS)
            at = slice(lo - owner * COLS, hi - owner * COLS)
            chunks[owner % 2, owner // 2, at] = block[lo - i * HALF : hi - i * HALF].astype(BF16)
            lo = hi
    pair_copy.start()
    pair_copy.wait_recv()

    def add_pair(i, carry):
        zsend[i] = (chunks[core, i].astype(F32) + paired[i].astype(F32)).astype(BF16)
        return carry

    lax.fori_loop(0, 8, add_pair, 0)

    def z_others(body):
        def turn(s, carry):
            body(lax.rem(z + s, 8))
            return carry

        lax.fori_loop(1, 8, turn, 0)

    z_others(lambda to: z_copy(to, z).start())
    others(lambda k: back_copy(me, k).wait_recv())
    sg_ref[...] = landed[...]
    z_others(lambda k: z_copy(k, k).wait_recv())
    zrecv[z] = zsend[z]
    summed = zrecv[0].astype(F32)
    for k in range(1, 8):
        summed += zrecv[k].astype(F32)
    padded = jnp.concatenate([summed, jnp.zeros((HALF - COLS, WIDE), F32)], axis=0).T
    out_ref[...] = padded[:OWN, :COLS]

    def finish(to):
        fac_copy(to, me).wait_send()
        push_copy(to, to, me).wait_send()
        square_copy(to, me).wait_send()
        back_copy(to, me).wait_send()

    others(finish)
    pair_copy.wait_send()
    z_others(lambda to: z_copy(to, z).wait_send())


def exchange(pushed, factors, terms, scale):
    vmem = pl.BlockSpec(memory_space=pltpu.VMEM)
    return pl.pallas_call(
        functools.partial(exchange_kernel, scale),
        out_shape=(jax.ShapeDtypeStruct((STATE, INNER), BF16), jax.ShapeDtypeStruct((OWN, COLS), F32)),
        in_specs=[vmem] * 6,
        out_specs=(vmem, vmem),
        scratch_shapes=[
            pltpu.VMEM((CTX, 16, HALFIN), BF16),
            pltpu.VMEM((CTX, 8, HALF), F32),
            pltpu.VMEM((16, HALFIN), F32),
            pltpu.VMEM((CTX, 8, HALFIN), F32),
            pltpu.VMEM((CTX, 16, HALFIN), BF16),
            pltpu.VMEM((STATE, INNER), BF16),
            pltpu.VMEM((CTX, 8, HALF), F32),
            pltpu.VMEM((8, HALF), F32),
            pltpu.VMEM((WIDE, MODEL), F32),
            pltpu.VMEM((2, 8, COLS, WIDE), BF16),
            pltpu.VMEM((8, COLS, WIDE), BF16),
            pltpu.VMEM((8, COLS, WIDE), BF16),
            pltpu.VMEM((8, COLS, WIDE), BF16),
        ]
        + [pltpu.SemaphoreType.DMA((CTX,))] * 8
        + [pltpu.SemaphoreType.DMA, pltpu.SemaphoreType.DMA]
        + [pltpu.SemaphoreType.DMA((8,))] * 2,
        compiler_params=params(collective_id=0, has_side_effects=True),
        cost_estimate=pl.CostEstimate(flops=10**8, bytes_accessed=50 * 10**6, transcendentals=0),
        name="exchange",
    )(pushed, factors, *terms)


def move(value, axis, step):
    def source(i):
        return (i // SIDE, i % SIDE)

    pairs = []
    for i in range(CTX):
        x, y = source(i)
        to = ((x + step) % SIDE) * SIDE + y if axis == 0 else x * SIDE + (y + step) % SIDE
        pairs.append((i, to))
    return lax.ppermute(value, "ctx", pairs)


def per_device(
    ssm_input,
    gate_input,
    input_map,
    output_map,
    step_size,
    log_rate,
    entry_state,
    norm_gain,
    out_weight,
    out_grad,
):
    examples = lax.axis_size("dp")
    me = lax.axis_index("ctx")
    y = me % SIDE
    ssm, gate, og = ssm_input[0], gate_input[0], out_grad[0]
    b, c = input_map[0], output_map[0]
    step = step_size.reshape(GROUPS, GROUP, TOK)
    rates = log_rate.reshape(GROUPS, GROUP, 1)
    state = entry_state.reshape(INNER, STATE)
    gain = norm_gain.reshape(1, INNER)
    padded = jnp.pad(out_weight, ((0, 32 - out_weight.shape[0]), (0, 0)))

    gated, r, gg, mean, gx, ox = gather(ssm, gate, step, rates, state, b, c, gain, padded, og)
    factor = jnp.exp(-jnp.exp(log_rate) * jnp.sum(step_size[0], axis=-1))
    factors = jnp.broadcast_to(jnp.pad(factor, (0, HALF - factor.shape[0]))[None], (8, HALF))
    partial = weight_partials(gx, ox)

    def chunk(s):
        return lax.dynamic_index_in_dim(partial, lax.rem(y + s, SIDE), axis=0, keepdims=False)

    terms = [chunk(0)] + [move(chunk(s), 1, s) for s in range(1, SIDE)]

    y_grad, pushed = norm_backward(gg, gated, gate, r, mean, gain, step, rates, c)
    scale = math.sqrt(INNER * MODEL / examples)
    state_grad, summed = exchange(pushed, factors, terms, scale)
    input_grad = scan_backward(y_grad, state_grad, step, rates, b, c)
    return (input_grad[None], summed)


def solution(mesh):
    placed = (
        P("dp", "ctx", None),
        P("dp", "ctx", None),
        P("dp", "ctx", None),
        P("dp", "ctx", None),
        P("dp", None, "ctx"),
        P(),
        P("dp", "ctx", None, None, None),
        P(),
        P(("dp", "ctx"), None),
        P("dp", "ctx", None),
    )
    return jax.shard_map(
        per_device,
        mesh=mesh,
        in_specs=placed,
        out_specs=(P("dp", "ctx", None), P("ctx", "dp")),
        check_vma=False,
    )
```

```python
import functools
import math

import jax
import jax.numpy as jnp
from jax import lax
from jax.experimental import pallas as pl
from jax.experimental.pallas import tpu as pltpu
from jax.sharding import PartitionSpec as P

NORM_EPS = 1e-05
CLIP_EPS = 1e-06
MESH = pl.DeviceIdType.MESH
F32 = jnp.float32
BF16 = jnp.bfloat16
HIGHEST = lax.Precision.HIGHEST

TOK = 256
HALF = 128
STATE = 128
HEADS = 80
GROUP = 10
LANES = 640
GROUPS = 8
INNER = 5120
MODEL = 1280
CAP = 80.0
SIDE = 4
CTX = 16
RING = 8
OWN = INNER // CTX
WIDE = 384
COLS = MODEL // 16
THIN = 32
EARLY = 3
VMEM_BYTES = 60 * 1024 * 1024


def dot(a, b):
    return jnp.dot(a, b, preferred_element_type=F32)


def dot_nt(a, b):
    return lax.dot_general(a, b, (((1,), (1,)), ((), ())), preferred_element_type=F32)


def rows_of(shape):
    return lax.broadcasted_iota(jnp.int32, shape, 0)


def lanes_of(shape):
    return lax.broadcasted_iota(jnp.int32, shape, 1)


def low_half():
    return lanes_of((TOK, HALF)) < HALF // 2


def pair_cols(columns, pair):
    return jnp.where(low_half(), columns[:, 2 * pair : 2 * pair + 1], columns[:, 2 * pair + 1 : 2 * pair + 2])


def split_pair(values):
    zero = jnp.zeros_like(values)
    return jnp.where(low_half(), values, zero), jnp.where(low_half(), zero, values)


def silu(gate):
    return gate / (1.0 + jnp.exp(-gate))


def lane_block(at, width):
    return pl.ds(pl.multiple_of(at * width, HALF), width)


def layer_kernel(
    scale,
    x_ref,
    z_ref,
    st_ref,
    lr_ref,
    s_ref,
    b_ref,
    c_ref,
    gain_ref,
    w_ref,
    og_ref,
    out_ref,
    grad_ref,
    steps,
    rates,
    cums,
    shifts,
    xbuf,
    sbuf,
    mixed,
    gated,
    coup,
    upper,
    acc,
    rms,
    turned,
    wpad,
    thin,
    full,
    gx,
    ox,
    partial,
    landing,
    relay,
    ybuf,
    term,
    square_own,
    squares,
    chunks,
    paired,
    zsend,
    zrecv,
    fac,
    facs,
    expanded,
    ct,
    pushed,
    arrived,
    running,
    back,
    landed,
    prelay,
    brelay,
    x_sem,
    s_sem,
    out_sem,
    w_send,
    w_recv,
    ring_send,
    ring_recv,
    wy_send,
    wy_recv,
    sib_send,
    sib_recv,
    o_send,
    o_recv,
    g_send,
    g_recv,
    y_send,
    y_recv,
    r_send,
    r_recv,
    yf_send,
    yf_recv,
    q_send,
    q_recv,
    pair_send,
    pair_recv,
    z_send,
    z_recv,
    f_send,
    f_recv,
    p_send,
    p_recv,
    b_send,
    b_recv,
    pr_recv,
    po_send,
    br_recv,
    bo_send,
):
    dp, me = lax.axis_index("dp"), lax.axis_index("ctx")
    core, z = lax.rem(dp, 2), lax.div(dp, 2)
    x, y = lax.div(me, SIDE), lax.rem(me, SIDE)
    partner = dp + 1 - 2 * core

    def remote(src, dst, send, recv, to):
        return pltpu.make_async_remote_copy(
            src_ref=src, dst_ref=dst, send_sem=send, recv_sem=recv, device_id=to, device_id_type=MESH
        )

    def others(body):
        def turn(s, carry):
            body(lax.rem(me + s, CTX))
            return carry

        lax.fori_loop(1, CTX, turn, 0)

    def z_others(body):
        def turn(s, carry):
            body(lax.rem(z + s, RING))
            return carry

        lax.fori_loop(1, RING, turn, 0)

    def load_group(at):
        slot = lax.rem(at, 2)
        return (
            pltpu.make_async_copy(x_ref.at[:, lane_block(at, LANES)], xbuf.at[slot], x_sem.at[slot]),
            pltpu.make_async_copy(s_ref.at[lane_block(at, LANES)], sbuf.at[slot], s_sem.at[slot]),
        )

    def store_group(at):
        slot = lax.rem(at, 2)
        return pltpu.make_async_copy(xbuf.at[slot], out_ref.at[:, lane_block(at, LANES)], out_sem.at[slot])

    for copy in load_group(0):
        copy.start()

    barrier = pltpu.get_barrier_semaphore()

    def greet(to):
        pl.semaphore_signal(barrier, inc=1, device_id=(dp, to), device_id_type=MESH)

    def greet_z(to):
        pl.semaphore_signal(barrier, inc=1, device_id=(2 * to + core, me), device_id_type=MESH)

    others(greet)
    z_others(greet_z)
    pl.semaphore_signal(barrier, inc=1, device_id=(partner, me), device_id_type=MESH)

    wide_w = jnp.concatenate([w_ref[...].astype(F32), jnp.zeros((THIN - OWN // CTX, MODEL), F32)], axis=0)
    wpad[...] = wide_w.astype(BF16)
    odd = lax.rem(y, 2)
    part_of = lax.div(me, RING)

    def thin_from(i):
        return remote(wpad, thin.at[i], w_send.at[i], w_recv.at[i], (dp, RING * odd + i))

    def thin_out(i):
        return SIDE * lax.div(i, 2) + 2 * lax.rem(i, 2) + part_of

    def thin_send(i):
        to = thin_out(i)
        return remote(wpad, thin.at[lax.rem(me, RING)], w_send.at[i], w_recv.at[lax.rem(me, RING)], (dp, to))

    def each_thin_out(body):
        def turn(i, carry):
            @pl.when(thin_out(i) != me)
            def _():
                body(i)

            return carry

        lax.fori_loop(0, RING, turn, 0)

    def block_part(at, which, part):
        row = pl.multiple_of(which * OWN + part * COLS, 16)
        return full.at[at, pl.ds(row, COLS)]

    def ring_copy(way, turn, half, at):
        slot = (way * 4 + turn) * 2 + half
        to = 2 * lax.rem(z + (1 if way == 0 else RING - 1), RING) + core
        block = block_part(at, core, 2 * odd + half)
        return remote(block, block, ring_send.at[slot], ring_recv.at[slot], (to, me))

    def side_copy(at, half, parity):
        to = (dp, x * SIDE + lax.rem(y + (1 if half == 0 else SIDE - 1), SIDE))
        block = block_part(at, core, 2 * parity + half)
        return remote(block, block, wy_send.at[at, half], wy_recv.at[at, half], to)

    def sib_copy(at, which, part):
        block = block_part(at, which, part)
        return remote(block, block, sib_send.at[at, part], sib_recv.at[at, part], (partner, me))

    def x_peer(s):
        return (dp, lax.rem(x + s, SIDE) * SIDE + y)

    def y_peer(s):
        return (dp, x * SIDE + lax.rem(y + s, SIDE))

    def o_copy(s, slot):
        return remote(og_ref, ox.at[slot], o_send.at[s], o_recv.at[s], x_peer(s))

    def o_relay(half, slot):
        block = ox.at[slot, pl.ds(half * HALF, HALF)]
        return remote(block, block, o_send.at[2 * half], o_recv.at[2 * half], x_peer(1 if half == 0 else 3))

    def turned_rows(s, half, count):
        to = lax.rem(x + s, SIDE)
        return turned.at[pl.ds(pl.multiple_of(to * MODEL + half * (MODEL // 2), HALF), count)]

    def g_copy(s, slot):
        return remote(turned_rows(s, 0, MODEL), gx.at[slot], g_send.at[s], g_recv.at[s], x_peer(s))

    def g_far(half):
        to = x_peer(1 if half == 0 else 3)
        return remote(turned_rows(2, half, MODEL // 2), relay.at[half], r_send.at[half], r_recv.at[half], to)

    def g_relay(half, slot):
        block = gx.at[slot, pl.ds(half * (MODEL // 2), MODEL // 2)]
        return remote(relay.at[half], block, g_send.at[2 * half], g_recv.at[2 * half], x_peer(1 if half == 0 else 3))

    def y_far(half):
        block = partial.at[2, pl.ds(half * (OWN // 2), OWN // 2)]
        return remote(block, ybuf.at[half], yf_send.at[half], yf_recv.at[half], y_peer(1 if half == 0 else 3))

    def y_near(side, half):
        rows = pl.ds(half * (OWN // 2), OWN // 2)
        s, slot = 1 + 2 * side, 2 * side + half
        return remote(partial.at[s, rows], landing.at[side, rows], y_send.at[slot], y_recv.at[slot], y_peer(s))

    def square_copy(to, slot):
        return remote(square_own, squares.at[slot], q_send.at[to], q_recv.at[slot], (dp, to))

    pair_copy = remote(chunks.at[1 - core], paired, pair_send, pair_recv, (partner, me))

    def z_copy(to, slot):
        return remote(zsend.at[to], zrecv.at[slot], z_send.at[to], z_recv.at[slot], (2 * to + core, me))

    def piece(ref, owner):
        row = pl.multiple_of(lax.div(owner, SIDE) * THIN, THIN)
        return ref.at[pl.ds(row, THIN), lane_block(lax.rem(owner, SIDE), MODEL)]

    def fac_copy(to, slot):
        return remote(fac, facs.at[slot], f_send.at[to], f_recv.at[slot], (dp, to))

    def push_copy(src, to, slot):
        return remote(piece(pushed, src), arrived.at[slot], p_send.at[to], p_recv.at[slot], (dp, to))

    def back_copy(to, owner):
        return remote(back.at[to], piece(landed, owner), b_send.at[to], b_recv.at[owner], (dp, to))


    for at in range(GROUPS):
        steps[at, :GROUP, :] = st_ref[at * GROUP : (at + 1) * GROUP, :]
    rate_rows = jnp.broadcast_to(jnp.exp(lr_ref[...]), (HALF, HEADS)).T
    for at in range(GROUPS):
        rates[at, :GROUP, :] = rate_rows[at * GROUP : (at + 1) * GROUP, :]
    square = (TOK, TOK)
    coup[...] = jnp.where(rows_of(square) >= lanes_of(square), dot_nt(c_ref[...], b_ref[...]), 0.0)
    upper[...] = jnp.where(rows_of(square) <= lanes_of(square), 1.0, 0.0).astype(F32)
    ct[...] = c_ref[...].astype(F32).T.astype(BF16)
    acc[...] = jnp.zeros_like(acc)
    fac[...] = jnp.zeros_like(fac)

    def forward(at, carry):
        slot = lax.rem(at, 2)

        @pl.when(at + 1 < GROUPS)
        def _():
            for copy in load_group(at + 1):
                copy.start()

        step = steps[at, :GROUP, :]
        drop = -(rates[at, :GROUP, :1] * step)
        cumulative = jnp.dot(drop, upper[...], preferred_element_type=F32, precision=HIGHEST)
        shifted = cumulative - jnp.log(step)
        cums[at, :GROUP, :] = cumulative
        shifts[at, :GROUP, :] = shifted
        columns = cumulative.T
        fac[pl.ds(at, 1), :GROUP] = jnp.exp(columns[TOK - 1 :, :])
        for copy in load_group(at):
            copy.wait()
        for pair in range(GROUP // 2):
            here = slice(pair * HALF, (pair + 1) * HALF)
            parts = split_pair(xbuf[slot, :, here])
            top = bottom = None
            for which in range(2):
                head = 2 * pair + which
                col = columns[:, head : head + 1]
                row = shifted[head : head + 1, :]
                m_top = jnp.exp(jnp.minimum(col[:HALF] - row[:, :HALF], CAP)) * coup[:HALF, :HALF]
                m_bot = jnp.exp(jnp.minimum(col[HALF:] - row, CAP)) * coup[HALF:, :]
                t = dot(m_top.astype(BF16), parts[which][:HALF])
                b = dot(m_bot.astype(BF16), parts[which])
                top = t if top is None else top + t
                bottom = b if bottom is None else bottom + b
            inside = jnp.concatenate([top, bottom], axis=0)
            carried = dot_nt(c_ref[...], sbuf[slot, here, :])
            value = inside + carried * jnp.exp(pair_cols(columns, pair))
            lanes = pl.ds(pl.multiple_of(at * LANES + pair * HALF, HALF), HALF)
            mix = value * silu(z_ref[:, lanes].astype(F32))
            mixed[at, :, here] = mix
            acc[...] += mix * mix
        return carry

    def arriving(turn, half):
        for way in (0, 1):
            if turn < 3 or half == way:
                yield way, lax.rem(z + (RING - turn - 1 if way == 0 else turn + 1), RING)

    def arrive(turn, half):
        for way, at in arriving(turn, half):
            ring_copy(way, turn, half, at).wait_recv()
            if turn < 2 or (turn == 2 and half == way):
                ring_copy(way, turn + 1, half, at).start()
            side_copy(at, half, odd).start()
            sib_copy(at, core, 2 * odd + half).start()

    def arrive_side(turn, half):
        for _, at in arriving(turn, half):
            side_copy(at, half, 1 - odd).wait_recv()
            sib_copy(at, core, 2 * (1 - odd) + half).start()

    lax.fori_loop(0, EARLY, forward, 0)
    pl.semaphore_wait(barrier, CTX - 1 + RING - 1 + 1)
    def far_route(to):
        tx, ty = lax.div(to, SIDE), lax.rem(to, SIDE)
        dx, dy = lax.rem(tx - x + SIDE, SIDE), lax.rem(ty - y + SIDE, SIDE)
        over_y = jnp.logical_and(dy == 2, lax.rem(dx, 2) == 1)
        over_x = jnp.logical_and(dx == 2, lax.rem(dy, 2) == 1)
        via = jnp.where(over_y, tx * SIDE + lax.rem(y + 3, SIDE), lax.rem(x + 3, SIDE) * SIDE + ty)
        slot = jnp.where(over_y, lax.div(dx, 2), 2 + lax.div(dy, 2))
        return jnp.logical_or(over_y, over_x), via, slot

    def hand_on(slot):
        source_x, source_y = ((3, 1), (1, 1), (1, 3), (1, 1))[slot]
        source = lax.rem(x + source_x, SIDE) * SIDE + lax.rem(y + source_y, SIDE)
        target = x * SIDE + lax.rem(y + 3, SIDE) if slot < 2 else lax.rem(x + 3, SIDE) * SIDE + y
        return source, target

    def push_far(to, via, slot):
        return remote(piece(pushed, to), prelay.at[slot], p_send.at[to], pr_recv.at[slot], (dp, via))

    def push_on(slot):
        source, target = hand_on(slot)
        return remote(prelay.at[slot], arrived.at[source], po_send.at[slot], p_recv.at[source], (dp, target))

    def push_far_wait(slot):
        return remote(prelay.at[slot], prelay.at[slot], po_send.at[slot], pr_recv.at[slot], (dp, hand_on(slot)[0]))

    def back_far(to, via, slot):
        return remote(back.at[to], brelay.at[slot], b_send.at[to], br_recv.at[slot], (dp, via))

    def back_on(slot):
        source, target = hand_on(slot)
        return remote(brelay.at[slot], piece(landed, source), bo_send.at[slot], b_recv.at[source], (dp, target))

    def back_far_wait(slot):
        return remote(brelay.at[slot], brelay.at[slot], bo_send.at[slot], br_recv.at[slot], (dp, hand_on(slot)[0]))

    def send_either(to, near_copy, far_copy):
        far, via, slot = far_route(to)

        @pl.when(jnp.logical_and(to != me, jnp.logical_not(far)))
        def _():
            near_copy(to).start()

        @pl.when(far)
        def _():
            far_copy(to, via, slot).start()

    each_thin_out(lambda i: thin_send(i).start())
    for s in (1, 3):
        o_copy(s, x).start()
    lax.fori_loop(EARLY, GROUPS, forward, 0)

    r = lax.rsqrt(jnp.sum(acc[...], axis=1, keepdims=True) * (1.0 / INNER) + NORM_EPS)
    rms[...] = jnp.broadcast_to(r, rms.shape)

    def finish_norm(at, carry):
        lanes = lane_block(at, LANES)
        normed = mixed[at] * rms[:, :1] * gain_ref[:, lanes]
        gated[at] = normed.astype(BF16)
        turned[lanes, :] = normed.T.astype(BF16)
        return carry

    lax.fori_loop(0, GROUPS, finish_norm, 0)

    for half in range(2):
        g_far(half).start()
    for s in (1, 3):
        g_copy(s, x).start()

    def wait_thin(i, carry):
        k = RING * odd + i

        @pl.when(k != me)
        def _():
            thin_from(i).wait_recv()

        return carry

    @pl.when(part_of == odd)
    def _():
        thin[lax.rem(me, RING)] = wpad[...]

    lax.fori_loop(0, RING, wait_thin, 0)
    rows = [thin[k][: OWN // CTX].astype(F32) for k in range(RING)]
    half_rows = pl.ds(pl.multiple_of(core * OWN + odd * (OWN // 2), 16), OWN // 2)
    full[z, half_rows] = jnp.concatenate(rows, axis=0).astype(BF16)
    for half in range(2):
        for way in range(2):
            ring_copy(way, 0, half, z).start()
        side_copy(z, half, odd).start()
        sib_copy(z, core, 2 * odd + half).start()

    left, right = lax.rem(x + 3, SIDE), lax.rem(x + 1, SIDE)
    gx[x] = turned[pl.ds(pl.multiple_of(x * MODEL, MODEL), MODEL), :]
    ox[x] = og_ref[...]
    others(lambda to: fac_copy(to, me).start())
    acc[...] = jnp.zeros_like(acc)

    def product(at):
        for part in range(SIDE):
            sib_copy(at, 1 - core, part).wait_recv()
        value = dot_nt(og_ref[...], full[at])
        mixed[at] = value
        both = value * gated[at].astype(F32)
        total = acc[...]
        for i in range(LANES // HALF):
            total += both[:, i * HALF : (i + 1) * HALF]
        acc[...] = total

    def weight_part(s):
        rows = pl.ds(pl.multiple_of(lax.rem(y + s, SIDE) * OWN, OWN), OWN)
        total = None
        for source in range(SIDE):
            part = dot(gx[source, rows, :], ox[source])
            total = part if total is None else total + part
        partial[s] = total.astype(BF16)

    def near(step):
        return lax.rem(z + step, RING)

    arrive(0, 0)
    arrive(0, 1)
    o_copy(1, left).wait_recv()
    o_relay(0, left).start()
    o_copy(3, right).wait_recv()
    o_relay(1, right).start()
    for half in range(2):
        side_copy(z, half, 1 - odd).wait_recv()
        sib_copy(z, core, 2 * (1 - odd) + half).start()
    arrive(1, 0)
    arrive_side(0, 0)
    product(z)
    arrive(1, 1)
    arrive_side(0, 1)
    for half in range(2):
        g_far(half).wait_recv()
        g_relay(half, left if half == 0 else right).start()
    arrive(2, 0)
    arrive_side(1, 0)
    product(near(1))
    product(near(7))
    arrive(2, 1)
    arrive_side(1, 1)
    arrive(3, 0)
    arrive_side(2, 0)
    product(near(2))
    product(near(6))
    arrive(3, 1)
    arrive_side(2, 1)
    arrive_side(3, 0)
    product(near(3))
    product(near(5))
    arrive_side(3, 1)
    product(near(4))
    mean = jnp.sum(acc[...], axis=1, keepdims=True) * (1.0 / INNER)
    acc[...] = jnp.broadcast_to(mean, acc.shape)

    def norm_back(at, carry):
        columns = cums[at].T
        for pair in range(GROUP // 2):
            here = slice(pair * HALF, (pair + 1) * HALF)
            lanes = pl.ds(pl.multiple_of(at * LANES + pair * HALF, HALF), HALF)
            gain = gain_ref[:, lanes]
            inner = gain * mixed[at, :, here] - gated[at, :, here].astype(F32) * (1.0 / gain) * acc[...]
            yg = silu(z_ref[:, lanes].astype(F32)) * rms[...] * inner
            gated[at, :, here] = yg.astype(BF16)
            weighted = (yg * jnp.exp(pair_cols(columns, pair))).astype(BF16)
            pushed[:, lanes] = dot(ct[...], weighted).astype(BF16)
        return carry

    for i in range(SIDE):
        quarter = lax.rem(y + 2 + i, SIDE)
        lax.fori_loop(2 * quarter, 2 * quarter + 2, norm_back, 0)

        def send_quarter(row, carry):
            send_either(SIDE * row + quarter, lambda to: push_copy(to, to, me), push_far)
            return carry

        lax.fori_loop(0, SIDE, send_quarter, 0)

    far = lax.rem(x + 2, SIDE)
    for half in range(2):
        o_relay(half, far).wait_recv()
        g_relay(half, far).wait_recv()
    g_copy(1, left).wait_recv()
    g_copy(3, right).wait_recv()
    weight_part(2)
    for half in range(2):
        y_far(half).start()
    weight_part(1)
    y_near(0, 1).start()
    weight_part(3)
    y_near(1, 0).start()
    weight_part(0)

    coup[...] = jnp.where(rows_of(square) <= lanes_of(square), dot_nt(b_ref[...], c_ref[...]), 0.0)

    def inside_back(at, carry):
        shifted = shifts[at]
        columns = shifted.T
        for pair in range(GROUP // 2):
            here = slice(pair * HALF, (pair + 1) * HALF)
            parts = split_pair(gated[at, :, here])
            top = bottom = None
            for which in range(2):
                head = 2 * pair + which
                col = columns[:, head : head + 1]
                row = cums[at, head : head + 1, :]
                m_top = jnp.exp(jnp.minimum(row - col[:HALF], CAP)) * coup[:HALF, :]
                m_bot = jnp.exp(jnp.minimum(row[:, HALF:] - col[HALF:], CAP)) * coup[HALF:, HALF:]
                t = dot(m_top.astype(BF16), parts[which])
                b = dot(m_bot.astype(BF16), parts[which][HALF:])
                top = t if top is None else top + t
                bottom = b if bottom is None else bottom + b
            mixed[at, :HALF, here] = top
            mixed[at, HALF:, here] = bottom
        return carry

    for slot in range(SIDE):
        push_far_wait(slot).wait_recv()
        push_on(slot).start()
    lax.fori_loop(0, 4, inside_back, 0)
    for half in range(2):
        y_far(half).wait_recv()
        at = slice(half * (OWN // 2), (half + 1) * (OWN // 2))
        added = partial[1 + 2 * half, at].astype(F32) + ybuf[half].astype(F32)
        partial[1 + 2 * half, at] = added.astype(BF16)
        y_near(half, half).start()
    lax.fori_loop(4, GROUPS, inside_back, 0)

    arrived[me] = piece(pushed, me)[...]
    facs[me] = fac[...]
    others(lambda k: fac_copy(k, k).wait_recv())
    shape = (HALF, LANES)
    hot = jnp.where(rows_of(shape) == lax.shift_right_logical(lanes_of(shape), 6), 1.0, 0.0).astype(F32)
    listed = jnp.concatenate([facs[k] for k in range(CTX)], axis=0)
    expanded[...] = jnp.dot(listed, hot, preferred_element_type=F32, precision=HIGHEST)
    running[...] = jnp.zeros_like(running)

    def chain(turn, carry):
        k = CTX - 1 - turn

        @pl.when(k != me)
        def _():
            push_copy(k, k, k).wait_recv()

        now = running[...]
        back[k] = now.astype(BF16)

        first = k * GROUPS + 2 * lax.rem(me, SIDE)
        factor = jnp.concatenate([expanded[pl.ds(first, 1), :], expanded[pl.ds(first + 1, 1), :]], axis=1)
        running[...] = factor * now + arrived[k].astype(F32)
        return carry

    lax.fori_loop(0, CTX, chain, 0)
    piece(landed, me)[...] = back[me]
    for side in range(2):
        for half in range(2):
            y_near(side, half).wait_recv()
    total = partial[0].astype(F32)
    for side in range(2):
        total += landing[side].astype(F32)
    term[:OWN, :] = total
    term[OWN:, :] = jnp.zeros((WIDE - OWN, MODEL), F32)
    folded = jnp.sum((total * total).reshape(OWN // 8, 8, MODEL), axis=0)
    part = folded[:, :HALF]
    for i in range(1, MODEL // HALF):
        part += folded[:, i * HALF : (i + 1) * HALF]
    square_own[...] = part
    others(lambda to: square_copy(to, me).start())

    def send_back(to, carry):
        send_either(to, lambda k: back_copy(k, me), back_far)
        return carry

    lax.fori_loop(0, CTX, send_back, 0)
    others(lambda k: square_copy(k, k).wait_recv())
    squares[me] = square_own[...]
    all_squares = squares[0]
    for k in range(1, CTX):
        all_squares += squares[k]
    whole = jnp.sum(jnp.sum(all_squares, axis=1, keepdims=True), axis=0, keepdims=True)
    clip = jnp.minimum(1.0, lax.rsqrt(whole + CLIP_EPS)) * scale
    for i in range(MODEL // HALF):
        block = (term[:, i * HALF : (i + 1) * HALF] * clip).T
        lo = i * HALF
        while lo < (i + 1) * HALF:
            owner = lo // COLS
            hi = min((i + 1) * HALF, (owner + 1) * COLS)
            at = slice(lo - owner * COLS, hi - owner * COLS)
            chunks[owner % 2, owner // 2, at] = block[lo - i * HALF : hi - i * HALF].astype(BF16)
            lo = hi
    pair_copy.start()

    def combine(at, carry):
        slot = lax.rem(at, 2)

        @pl.when(at >= 2)
        def _():
            store_group(at - 2).wait()

        last = (cums[at][:, TOK - 1 :] - shifts[at]).T
        ended = dot(b_ref[...], landed[:, lane_block(at, LANES)])
        for pair in range(GROUP // 2):
            here = slice(pair * HALF, (pair + 1) * HALF)
            value = mixed[at, :, here] + ended[:, here] * jnp.exp(pair_cols(last, pair))
            xbuf[slot, :, here] = value.astype(BF16)
        store_group(at).start()
        return carry

    for slot in range(SIDE):
        back_far_wait(slot).wait_recv()
        back_on(slot).start()
    pair_copy.wait_recv()

    def add_pair(i, carry):
        zsend[i] = (chunks[core, i].astype(F32) + paired[i].astype(F32)).astype(BF16)
        return carry

    lax.fori_loop(0, RING, add_pair, 0)
    z_others(lambda to: z_copy(to, z).start())
    others(lambda k: back_copy(me, k).wait_recv())
    lax.fori_loop(0, GROUPS, combine, 0)
    z_others(lambda k: z_copy(k, k).wait_recv())
    zrecv[z] = zsend[z]
    summed = zrecv[0].astype(F32)
    for k in range(1, RING):
        summed += zrecv[k].astype(F32)
    grad_ref[...] = summed[:, :OWN]

    store_group(GROUPS - 2).wait()
    store_group(GROUPS - 1).wait()

    def finish(to):
        fac_copy(to, me).wait_send()
        push_copy(to, to, me).wait_send()
        square_copy(to, me).wait_send()
        back_copy(to, me).wait_send()

    others(finish)
    pair_copy.wait_send()
    z_others(lambda to: z_copy(to, z).wait_send())
    each_thin_out(lambda i: thin_send(i).wait_send())
    for s in (1, 3):
        o_copy(s, x).wait_send()
        g_copy(s, x).wait_send()
    for half in range(2):
        o_relay(half, left if half == 0 else right).wait_send()
        g_far(half).wait_send()
        g_relay(half, left if half == 0 else right).wait_send()
        y_far(half).wait_send()
        for side in range(2):
            y_near(side, half).wait_send()
    for turn in range(4):
        for half in range(2):
            for way in range(2):
                if turn == 3 and half != way:
                    continue
                at = lax.rem(z + (RING - turn if way == 0 else turn), RING)
                ring_copy(way, turn, half, at).wait_send()

    for slot in range(SIDE):
        push_on(slot).wait_send()
        back_on(slot).wait_send()

    def finish_sib(at, carry):
        for part in range(SIDE):
            sib_copy(at, core, part).wait_send()
        return carry

    lax.fori_loop(0, RING, finish_sib, 0)

    def finish_side(at):
        for half in range(2):
            side_copy(at, half, odd).wait_send()

    z_others(finish_side)
    finish_side(z)


def layer(scale, *operands):
    vmem = pl.BlockSpec(memory_space=pltpu.VMEM)
    hbm = pl.BlockSpec(memory_space=pl.ANY)
    dma = pltpu.SemaphoreType.DMA
    ram = pltpu.VMEM
    return pl.pallas_call(
        functools.partial(layer_kernel, scale),
        out_shape=(jax.ShapeDtypeStruct((TOK, INNER), BF16), jax.ShapeDtypeStruct((COLS, OWN), F32)),
        in_specs=[hbm, vmem, vmem, vmem, hbm] + [vmem] * 5,
        out_specs=(hbm, vmem),
        scratch_shapes=[
            ram((GROUPS, 16, TOK), F32),
            ram((GROUPS, 16, HALF), F32),
            ram((GROUPS, 16, TOK), F32),
            ram((GROUPS, 16, TOK), F32),
            ram((2, TOK, LANES), BF16),
            ram((2, LANES, STATE), BF16),
            ram((GROUPS, TOK, LANES), F32),
            ram((GROUPS, TOK, LANES), BF16),
            ram((TOK, TOK), F32),
            ram((TOK, TOK), F32),
            ram((TOK, HALF), F32),
            ram((TOK, HALF), F32),
            ram((INNER, TOK), BF16),
            ram((THIN, MODEL), BF16),
            ram((RING, THIN, MODEL), BF16),
            ram((RING, 2 * OWN, MODEL), BF16),
            ram((SIDE, MODEL, TOK), BF16),
            ram((SIDE, TOK, MODEL), BF16),
            ram((SIDE, OWN, MODEL), BF16),
            ram((2, OWN, MODEL), BF16),
            ram((2, MODEL // 2, TOK), BF16),
            ram((2, OWN // 2, MODEL), BF16),
            ram((WIDE, MODEL), F32),
            ram((8, HALF), F32),
            ram((CTX, 8, HALF), F32),
            ram((2, RING, COLS, WIDE), BF16),
            ram((RING, COLS, WIDE), BF16),
            ram((RING, COLS, WIDE), BF16),
            ram((RING, COLS, WIDE), BF16),
            ram((8, HALF), F32),
            ram((CTX, 8, HALF), F32),
            ram((HALF, LANES), F32),
            ram((STATE, TOK), BF16),
            ram((STATE, INNER), BF16),
            ram((CTX, THIN, MODEL), BF16),
            ram((THIN, MODEL), F32),
            ram((CTX, THIN, MODEL), BF16),
            ram((STATE, INNER), BF16),
            ram((SIDE, THIN, MODEL), BF16),
            ram((SIDE, THIN, MODEL), BF16),
        ]
        + [dma((2,))] * 3
        + [dma((RING,))] * 2
        + [dma((16,))] * 2
        + [dma((RING, 2))] * 2
        + [dma((RING, SIDE))] * 2
        + [dma((SIDE,))] * 6
        + [dma((2,))] * 4
        + [dma((CTX,))] * 2
        + [dma, dma]
        + [dma((RING,))] * 2
        + [dma((CTX,))] * 6
        + [dma((SIDE,))] * 4,
        compiler_params=pltpu.CompilerParams(
            collective_id=0, has_side_effects=True, vmem_limit_bytes=VMEM_BYTES
        ),
        cost_estimate=pl.CostEstimate(flops=14 * 10**9, bytes_accessed=100 * 10**6, transcendentals=3 * 10**7),
        name="layer",
    )(*operands)


def per_device(
    ssm_input,
    gate_input,
    input_map,
    output_map,
    step_size,
    log_rate,
    entry_state,
    norm_gain,
    out_weight,
    out_grad,
):
    scale = math.sqrt(INNER * MODEL / lax.axis_size("dp"))
    input_grad, summed = layer(
        scale,
        ssm_input[0],
        gate_input[0],
        step_size[0],
        log_rate.reshape(1, HEADS),
        entry_state.reshape(INNER, STATE),
        input_map[0],
        output_map[0],
        norm_gain.reshape(1, INNER),
        out_weight,
        out_grad[0],
    )
    return (input_grad[None], summed.T)


def solution(mesh):
    placed = (
        P("dp", "ctx", None),
        P("dp", "ctx", None),
        P("dp", "ctx", None),
        P("dp", "ctx", None),
        P("dp", None, "ctx"),
        P(),
        P("dp", "ctx", None, None, None),
        P(),
        P(("dp", "ctx"), None),
        P("dp", "ctx", None),
    )
    return jax.shard_map(
        per_device,
        mesh=mesh,
        in_specs=placed,
        out_specs=(P("dp", "ctx", None), P("ctx", "dp")),
        check_vma=False,
    )
```

```python
import functools
import math

import jax
import jax.numpy as jnp
from jax import lax
from jax.experimental import pallas as pl
from jax.experimental.pallas import tpu as pltpu
from jax.sharding import PartitionSpec as P

NORM_EPS = 1e-05
CLIP_EPS = 1e-06
MESH = pl.DeviceIdType.MESH
F32 = jnp.float32
BF16 = jnp.bfloat16
HIGHEST = lax.Precision.HIGHEST

TOK = 256
HALF = 128
STATE = 128
HEADS = 80
GROUP = 10
LANES = 640
GROUPS = 8
INNER = 5120
MODEL = 1280
CAP = 80.0
SIDE = 4
CTX = 16
RING = 8
OWN = INNER // CTX
WIDE = 384
COLS = MODEL // 16
THIN = 32
EARLY = 3
THINAT = 6
VMEM_BYTES = 60 * 1024 * 1024


def dot(a, b):
    return jnp.dot(a, b, preferred_element_type=F32)


def dot_nt(a, b):
    return lax.dot_general(a, b, (((1,), (1,)), ((), ())), preferred_element_type=F32)


def rows_of(shape):
    return lax.broadcasted_iota(jnp.int32, shape, 0)


def lanes_of(shape):
    return lax.broadcasted_iota(jnp.int32, shape, 1)


def low_half():
    return lanes_of((TOK, HALF)) < HALF // 2


def pair_cols(columns, pair):
    return jnp.where(low_half(), columns[:, 2 * pair : 2 * pair + 1], columns[:, 2 * pair + 1 : 2 * pair + 2])


def split_pair(values):
    zero = jnp.zeros_like(values)
    return jnp.where(low_half(), values, zero), jnp.where(low_half(), zero, values)


def silu(gate):
    return gate / (1.0 + jnp.exp(-gate))


def lane_block(at, width):
    return pl.ds(pl.multiple_of(at * width, HALF), width)


def layer_kernel(
    scale,
    x_ref,
    z_hbm,
    st_ref,
    lr_ref,
    s_ref,
    b_ref,
    c_ref,
    gain_ref,
    w_ref,
    og_ref,
    out_ref,
    grad_ref,
    steps,
    rates,
    cums,
    shifts,
    xbuf,
    sbuf,
    z_ref,
    mixed,
    gated,
    coup,
    upper,
    acc,
    rms,
    turned,
    wpad,
    thin,
    full,
    gx,
    ox,
    partial,
    landing,
    relay,
    ybuf,
    term,
    square_own,
    squares,
    chunks,
    paired,
    zsend,
    zrecv,
    fac,
    facs,
    expanded,
    ct,
    pushed,
    arrived,
    running,
    back,
    landed,
    gate_sem,
    x_sem,
    s_sem,
    out_sem,
    w_send,
    w_recv,
    ring_send,
    ring_recv,
    wy_send,
    wy_recv,
    sib_send,
    sib_recv,
    o_send,
    o_recv,
    g_send,
    g_recv,
    y_send,
    y_recv,
    r_send,
    r_recv,
    yf_send,
    yf_recv,
    q_send,
    q_recv,
    pair_send,
    pair_recv,
    z_send,
    z_recv,
    f_send,
    f_recv,
    p_send,
    p_recv,
    b_send,
    b_recv,
):
    dp, me = lax.axis_index("dp"), lax.axis_index("ctx")
    core, z = lax.rem(dp, 2), lax.div(dp, 2)
    x, y = lax.div(me, SIDE), lax.rem(me, SIDE)
    partner = dp + 1 - 2 * core
    first = core == 0
    a, r = jnp.where(first, x, y), jnp.where(first, y, x)

    def over_x(s):
        return lax.rem(x + s, SIDE) * SIDE + y

    def over_y(s):
        return x * SIDE + lax.rem(y + s, SIDE)

    def a_peer(s):
        return (dp, jnp.where(first, over_x(s), over_y(s)))

    def r_peer(s):
        return (dp, jnp.where(first, over_y(s), over_x(s)))

    def remote(src, dst, send, recv, to):
        return pltpu.make_async_remote_copy(
            src_ref=src, dst_ref=dst, send_sem=send, recv_sem=recv, device_id=to, device_id_type=MESH
        )

    def others(body):
        def turn(s, carry):
            body(lax.rem(me + s, CTX))
            return carry

        lax.fori_loop(1, CTX, turn, 0)

    def z_others(body):
        def turn(s, carry):
            body(lax.rem(z + s, RING))
            return carry

        lax.fori_loop(1, RING, turn, 0)

    def load_group(at):
        slot = lax.rem(at, 2)
        return (
            pltpu.make_async_copy(x_ref.at[:, lane_block(at, LANES)], xbuf.at[slot], x_sem.at[slot]),
            pltpu.make_async_copy(s_ref.at[lane_block(at, LANES)], sbuf.at[slot], s_sem.at[slot]),
        )

    def store_group(at, slot):
        return pltpu.make_async_copy(xbuf.at[slot], out_ref.at[:, lane_block(at, LANES)], out_sem.at[slot])

    def load_gate(at):
        lanes = lane_block(at, LANES)
        return pltpu.make_async_copy(z_hbm.at[:, lanes], z_ref.at[:, lanes], gate_sem.at[at])

    for copy in load_group(0):
        copy.start()
    for at in range(GROUPS):
        load_gate(at).start()

    barrier = pltpu.get_barrier_semaphore()

    def greet(to):
        pl.semaphore_signal(barrier, inc=1, device_id=(dp, to), device_id_type=MESH)

    def greet_z(to):
        pl.semaphore_signal(barrier, inc=1, device_id=(2 * to + core, me), device_id_type=MESH)

    others(greet)
    z_others(greet_z)
    pl.semaphore_signal(barrier, inc=1, device_id=(partner, me), device_id_type=MESH)

    weights = w_ref[...].astype(F32)
    wpad[:, :MODEL] = weights[:16].astype(BF16)
    rest = [weights[16:, WIDE * i : min(WIDE * (i + 1), MODEL)] for i in range(SIDE)]
    rest[-1] = jnp.concatenate([rest[-1], jnp.zeros((4, WIDE - rest[-1].shape[1]), F32)], axis=1)
    wpad[:, MODEL:] = jnp.concatenate(rest, axis=0).astype(BF16)

    odd = lax.rem(r, 2)
    part_of = lax.div(me, RING)

    def thin_from(i):
        return remote(wpad, thin.at[i], w_send.at[i], w_recv.at[i], (dp, RING * odd + i))

    def thin_out(i):
        along, across = 2 * lax.rem(i, 2) + part_of, lax.div(i, 2)
        return jnp.where(first, SIDE * across + along, SIDE * along + across)

    def thin_send(i):
        to = thin_out(i)
        return remote(wpad, thin.at[lax.rem(me, RING)], w_send.at[i], w_recv.at[lax.rem(me, RING)], (dp, to))

    def each_thin_out(body):
        def turn(i, carry):
            @pl.when(thin_out(i) != me)
            def _():
                body(i)

            return carry

        lax.fori_loop(0, RING, turn, 0)

    def block_part(at, which, part):
        row = pl.multiple_of(which * OWN + part * COLS, 16)
        return full.at[at, pl.ds(row, COLS)]

    def ring_copy(way, turn, half, at):
        slot = (way * 4 + turn) * 2 + half
        to = 2 * lax.rem(z + (1 if way == 0 else RING - 1), RING) + core
        block = block_part(at, core, 2 * odd + half)
        return remote(block, block, ring_send.at[slot], ring_recv.at[slot], (to, me))

    def side_copy(at, half, parity):
        block = block_part(at, core, 2 * parity + half)
        to = r_peer(1 if half == 0 else 3)
        return remote(block, block, wy_send.at[at, half], wy_recv.at[at, half], to)

    def sib_copy(at, which, part):
        block = block_part(at, which, part)
        return remote(block, block, sib_send.at[at, part], sib_recv.at[at, part], (partner, me))

    def o_copy(s, slot):
        return remote(og_ref, ox.at[slot], o_send.at[s], o_recv.at[s], a_peer(s))

    def o_relay(half, slot):
        block = ox.at[slot, pl.ds(half * HALF, HALF)]
        return remote(block, block, o_send.at[2 * half], o_recv.at[2 * half], a_peer(1 if half == 0 else 3))

    def turned_rows(s, half, count):
        to = lax.rem(a + s, SIDE)
        return turned.at[pl.ds(pl.multiple_of(to * MODEL + half * (MODEL // 2), HALF), count)]

    def g_copy(s, slot):
        return remote(turned_rows(s, 0, MODEL), gx.at[slot], g_send.at[s], g_recv.at[s], a_peer(s))

    def g_far(half):
        to = a_peer(1 if half == 0 else 3)
        return remote(turned_rows(2, half, MODEL // 2), relay.at[half], r_send.at[half], r_recv.at[half], to)

    def g_relay(half, slot):
        block = gx.at[slot, pl.ds(half * (MODEL // 2), MODEL // 2)]
        return remote(relay.at[half], block, g_send.at[2 * half], g_recv.at[2 * half], a_peer(1 if half == 0 else 3))

    def y_far(half):
        block = partial.at[2, pl.ds(half * (OWN // 2), OWN // 2)]
        return remote(block, ybuf.at[half], yf_send.at[half], yf_recv.at[half], r_peer(1 if half == 0 else 3))

    def y_near(side, half):
        rows = pl.ds(half * (OWN // 2), OWN // 2)
        s, slot = 1 + 2 * side, 2 * side + half
        return remote(partial.at[s, rows], landing.at[side, rows], y_send.at[slot], y_recv.at[slot], r_peer(s))

    def square_copy(to, slot):
        return remote(square_own, squares.at[slot], q_send.at[to], q_recv.at[slot], (dp, to))

    pair_copy = remote(chunks.at[1 - core], paired, pair_send, pair_recv, (partner, me))

    def z_copy(to, slot):
        return remote(zsend.at[to], zrecv.at[slot], z_send.at[to], z_recv.at[slot], (2 * to + core, me))

    def piece(ref, owner):
        row = pl.multiple_of(lax.div(owner, SIDE) * THIN, THIN)
        return ref.at[pl.ds(row, THIN), lane_block(lax.rem(owner, SIDE), MODEL)]

    def fac_copy(to, slot):
        return remote(fac, facs.at[slot], f_send.at[to], f_recv.at[slot], (dp, to))

    def push_copy(src, to, slot):
        return remote(piece(pushed, src), arrived.at[slot], p_send.at[to], p_recv.at[slot], (dp, to))

    def back_copy(to, owner):
        return remote(back.at[to], piece(landed, owner), b_send.at[to], b_recv.at[owner], (dp, to))


    for at in range(GROUPS):
        steps[at, :GROUP, :] = st_ref[at * GROUP : (at + 1) * GROUP, :]
    rate_rows = jnp.broadcast_to(jnp.exp(lr_ref[...]), (HALF, HEADS)).T
    for at in range(GROUPS):
        rates[at, :GROUP, :] = rate_rows[at * GROUP : (at + 1) * GROUP, :]
    square = (TOK, TOK)
    coup[...] = jnp.where(rows_of(square) >= lanes_of(square), dot_nt(c_ref[...], b_ref[...]), 0.0)
    upper[...] = jnp.where(rows_of(square) <= lanes_of(square), 1.0, 0.0).astype(F32)
    ct[...] = c_ref[...].astype(F32).T.astype(BF16)
    acc[...] = jnp.zeros_like(acc)
    fac[...] = jnp.zeros_like(fac)

    def forward(at, carry):
        slot = lax.rem(at, 2)

        @pl.when(at + 1 < GROUPS)
        def _():
            for copy in load_group(at + 1):
                copy.start()

        step = steps[at, :GROUP, :]
        drop = -(rates[at, :GROUP, :1] * step)
        cumulative = jnp.dot(drop, upper[...], preferred_element_type=F32, precision=HIGHEST)
        shifted = cumulative - jnp.log(step)
        cums[at, :GROUP, :] = cumulative
        shifts[at, :GROUP, :] = shifted
        columns = cumulative.T
        fac[pl.ds(at, 1), :GROUP] = jnp.exp(columns[TOK - 1 :, :])
        for copy in load_group(at):
            copy.wait()
        load_gate(at).wait()
        for pair in range(GROUP // 2):
            here = slice(pair * HALF, (pair + 1) * HALF)
            parts = split_pair(xbuf[slot, :, here])
            top = bottom = None
            for which in range(2):
                head = 2 * pair + which
                col = columns[:, head : head + 1]
                row = shifted[head : head + 1, :]
                m_top = jnp.exp(jnp.minimum(col[:HALF] - row[:, :HALF], CAP)) * coup[:HALF, :HALF]
                m_bot = jnp.exp(jnp.minimum(col[HALF:] - row, CAP)) * coup[HALF:, :]
                t = dot(m_top.astype(BF16), parts[which][:HALF])
                b = dot(m_bot.astype(BF16), parts[which])
                top = t if top is None else top + t
                bottom = b if bottom is None else bottom + b
            inside = jnp.concatenate([top, bottom], axis=0)
            carried = dot_nt(c_ref[...], sbuf[slot, here, :])
            value = inside + carried * jnp.exp(pair_cols(columns, pair))
            lanes = pl.ds(pl.multiple_of(at * LANES + pair * HALF, HALF), HALF)
            mix = value * silu(z_ref[:, lanes].astype(F32))
            mixed[at, :, here] = mix
            acc[...] += mix * mix
        return carry

    def arriving(turn, half):
        for way in (0, 1):
            if turn < 3 or half == way:
                yield way, lax.rem(z + (RING - turn - 1 if way == 0 else turn + 1), RING)

    def arrive(turn, half):
        for way, at in arriving(turn, half):
            ring_copy(way, turn, half, at).wait_recv()
            if turn < 2 or (turn == 2 and half == way):
                ring_copy(way, turn + 1, half, at).start()
            side_copy(at, half, odd).start()
            sib_copy(at, core, 2 * odd + half).start()

    def arrive_side(turn, half):
        for _, at in arriving(turn, half):
            side_copy(at, half, 1 - odd).wait_recv()
            sib_copy(at, core, 2 * (1 - odd) + half).start()

    lax.fori_loop(0, EARLY, forward, 0)
    pl.semaphore_wait(barrier, CTX - 1 + RING - 1 + 1)
    def push_to(to):
        @pl.when(to != me)
        def _():
            push_copy(to, to, me).start()

    each_thin_out(lambda i: thin_send(i).start())
    lax.fori_loop(EARLY, THINAT, forward, 0)

    def wait_thin(i, carry):
        k = RING * odd + i

        @pl.when(k != me)
        def _():
            thin_from(i).wait_recv()

        return carry

    @pl.when(part_of == odd)
    def _():
        thin[lax.rem(me, RING)] = wpad[...]

    lax.fori_loop(0, RING, wait_thin, 0)
    rows = []
    for k in range(RING):
        value = thin[k].astype(F32)
        rest = [value[4 * i : 4 * i + 4, MODEL:] for i in range(SIDE)]
        rows += [value[:, :MODEL], jnp.concatenate(rest, axis=1)[:, :MODEL]]
    half_rows = pl.ds(pl.multiple_of(core * OWN + odd * (OWN // 2), 16), OWN // 2)
    full[z, half_rows] = jnp.concatenate(rows, axis=0).astype(BF16)
    for half in range(2):
        for way in range(2):
            ring_copy(way, 0, half, z).start()
        side_copy(z, half, odd).start()
        sib_copy(z, core, 2 * odd + half).start()
    for s in (1, 3):
        o_copy(s, a).start()
    lax.fori_loop(THINAT, GROUPS, forward, 0)

    inverse = lax.rsqrt(jnp.sum(acc[...], axis=1, keepdims=True) * (1.0 / INNER) + NORM_EPS)
    rms[...] = jnp.broadcast_to(inverse, rms.shape)

    def finish_norm(at, carry):
        lanes = lane_block(at, LANES)
        normed = mixed[at] * rms[:, :1] * gain_ref[:, lanes]
        gated[at] = normed.astype(BF16)
        rows = normed.T.astype(BF16)
        for which in range(2):
            block = 2 * at + which
            place = jnp.where(first, block, SIDE * lax.rem(block, SIDE) + lax.div(block, SIDE))
            turned[pl.ds(pl.multiple_of(place * OWN, OWN), OWN), :] = rows[which * OWN : (which + 1) * OWN]
        return carry

    lax.fori_loop(0, GROUPS, finish_norm, 0)

    for half in range(2):
        g_far(half).start()
    for s in (1, 3):
        g_copy(s, a).start()

    left, right = lax.rem(a + 3, SIDE), lax.rem(a + 1, SIDE)
    gx[a] = turned[pl.ds(pl.multiple_of(a * MODEL, MODEL), MODEL), :]
    ox[a] = og_ref[...]
    others(lambda to: fac_copy(to, me).start())
    acc[...] = jnp.zeros_like(acc)

    def product(at):
        for part in range(SIDE):
            sib_copy(at, 1 - core, part).wait_recv()
        value = dot_nt(og_ref[...], full[at])
        mixed[at] = value
        both = value * gated[at].astype(F32)
        total = acc[...]
        for i in range(LANES // HALF):
            total += both[:, i * HALF : (i + 1) * HALF]
        acc[...] = total

    def weight_part(s):
        rows = pl.ds(pl.multiple_of(lax.rem(r + s, SIDE) * OWN, OWN), OWN)
        total = None
        for source in range(SIDE):
            part = dot(gx[source, rows, :], ox[source])
            total = part if total is None else total + part
        partial[s] = total.astype(BF16)

    def near(step):
        return lax.rem(z + step, RING)

    arrive(0, 0)
    arrive(0, 1)
    o_copy(1, left).wait_recv()
    o_relay(0, left).start()
    o_copy(3, right).wait_recv()
    o_relay(1, right).start()
    for half in range(2):
        side_copy(z, half, 1 - odd).wait_recv()
        sib_copy(z, core, 2 * (1 - odd) + half).start()
    arrive(1, 0)
    arrive_side(0, 0)
    product(z)
    arrive(1, 1)
    arrive_side(0, 1)
    for half in range(2):
        g_far(half).wait_recv()
        g_relay(half, left if half == 0 else right).start()
    arrive(2, 0)
    arrive_side(1, 0)
    product(near(1))
    product(near(7))
    arrive(2, 1)
    arrive_side(1, 1)
    arrive(3, 0)
    arrive_side(2, 0)
    product(near(2))
    product(near(6))
    arrive(3, 1)
    arrive_side(2, 1)
    arrive_side(3, 0)
    product(near(3))
    product(near(5))
    far = lax.rem(a + 2, SIDE)
    for half in range(2):
        o_relay(half, far).wait_recv()
        g_relay(half, far).wait_recv()
    g_copy(1, left).wait_recv()
    g_copy(3, right).wait_recv()
    weight_part(2)
    for half in range(2):
        y_far(half).start()
    weight_part(1)
    y_near(0, 1).start()
    weight_part(3)
    y_near(1, 0).start()
    arrive_side(3, 1)
    product(near(4))
    weight_part(0)
    for half in range(2):
        y_far(half).wait_recv()
        at = slice(half * (OWN // 2), (half + 1) * (OWN // 2))
        added = partial[1 + 2 * half, at].astype(F32) + ybuf[half].astype(F32)
        partial[1 + 2 * half, at] = added.astype(BF16)
        y_near(half, half).start()
    mean = jnp.sum(acc[...], axis=1, keepdims=True) * (1.0 / INNER)
    acc[...] = jnp.broadcast_to(mean, acc.shape)

    def norm_back(at, carry):
        columns = cums[at].T
        for pair in range(GROUP // 2):
            here = slice(pair * HALF, (pair + 1) * HALF)
            lanes = pl.ds(pl.multiple_of(at * LANES + pair * HALF, HALF), HALF)
            gain = gain_ref[:, lanes]
            inner = gain * mixed[at, :, here] - gated[at, :, here].astype(F32) * (1.0 / gain) * acc[...]
            yg = silu(z_ref[:, lanes].astype(F32)) * rms[...] * inner
            gated[at, :, here] = yg.astype(BF16)
            weighted = (yg * jnp.exp(pair_cols(columns, pair))).astype(BF16)
            pushed[:, lanes] = dot(ct[...], weighted).astype(BF16)
        return carry

    for shift in (2, 1, 3, 0):
        quarter = lax.rem(y + shift, SIDE)
        lax.fori_loop(2 * quarter, 2 * quarter + 2, norm_back, 0)
        for row in range(SIDE):
            push_to(SIDE * lax.rem(x + (2, 1, 3, 0)[row], SIDE) + quarter)

    coup[...] = jnp.where(rows_of(square) <= lanes_of(square), dot_nt(b_ref[...], c_ref[...]), 0.0)

    def inside_back(at, carry):
        shifted = shifts[at]
        columns = shifted.T
        for pair in range(GROUP // 2):
            here = slice(pair * HALF, (pair + 1) * HALF)
            parts = split_pair(gated[at, :, here])
            top = bottom = None
            for which in range(2):
                head = 2 * pair + which
                col = columns[:, head : head + 1]
                row = cums[at, head : head + 1, :]
                m_top = jnp.exp(jnp.minimum(row - col[:HALF], CAP)) * coup[:HALF, :]
                m_bot = jnp.exp(jnp.minimum(row[:, HALF:] - col[HALF:], CAP)) * coup[HALF:, HALF:]
                t = dot(m_top.astype(BF16), parts[which])
                b = dot(m_bot.astype(BF16), parts[which][HALF:])
                top = t if top is None else top + t
                bottom = b if bottom is None else bottom + b
            mixed[at, :HALF, here] = top
            mixed[at, HALF:, here] = bottom
        return carry

    lax.fori_loop(0, 4, inside_back, 0)
    lax.fori_loop(4, GROUPS, inside_back, 0)
    for side in range(2):
        for half in range(2):
            y_near(side, half).wait_recv()
    total = partial[0].astype(F32)
    for side in range(2):
        total += landing[side].astype(F32)
    term[:OWN, :] = total
    term[OWN:, :] = jnp.zeros((WIDE - OWN, MODEL), F32)
    folded = jnp.sum((total * total).reshape(OWN // 8, 8, MODEL), axis=0)
    part = folded[:, :HALF]
    for i in range(1, MODEL // HALF):
        part += folded[:, i * HALF : (i + 1) * HALF]
    square_own[...] = part
    others(lambda to: square_copy(to, me).start())

    arrived[me] = piece(pushed, me)[...]
    facs[me] = fac[...]
    others(lambda k: fac_copy(k, k).wait_recv())
    shape = (HALF, LANES)
    hot = jnp.where(rows_of(shape) == lax.shift_right_logical(lanes_of(shape), 6), 1.0, 0.0).astype(F32)
    listed = jnp.concatenate([facs[k] for k in range(CTX)], axis=0)
    expanded[...] = jnp.dot(listed, hot, preferred_element_type=F32, precision=HIGHEST)
    running[...] = jnp.zeros_like(running)

    def chain(turn, carry):
        k = CTX - 1 - turn

        @pl.when(k != me)
        def _():
            push_copy(k, k, k).wait_recv()

        now = running[...]
        back[k] = now.astype(BF16)

        @pl.when(k != me)
        def _():
            back_copy(k, me).start()

        first = k * GROUPS + 2 * lax.rem(me, SIDE)
        factor = jnp.concatenate([expanded[pl.ds(first, 1), :], expanded[pl.ds(first + 1, 1), :]], axis=1)
        running[...] = factor * now + arrived[k].astype(F32)
        return carry

    lax.fori_loop(0, CTX, chain, 0)
    piece(landed, me)[...] = back[me]
    others(lambda k: square_copy(k, k).wait_recv())
    squares[me] = square_own[...]
    all_squares = squares[0]
    for k in range(1, CTX):
        all_squares += squares[k]
    whole = jnp.sum(jnp.sum(all_squares, axis=1, keepdims=True), axis=0, keepdims=True)
    clip = jnp.minimum(1.0, lax.rsqrt(whole + CLIP_EPS)) * scale
    for i in range(MODEL // HALF):
        block = (term[:, i * HALF : (i + 1) * HALF] * clip).T
        lo = i * HALF
        while lo < (i + 1) * HALF:
            owner = lo // COLS
            hi = min((i + 1) * HALF, (owner + 1) * COLS)
            at = slice(lo - owner * COLS, hi - owner * COLS)
            chunks[owner % 2, owner // 2, at] = block[lo - i * HALF : hi - i * HALF].astype(BF16)
            lo = hi
    pair_copy.start()

    def combine(at, count):
        slot = count % 2
        if count >= 2:
            store_group(at, slot).wait()
        last = (cums[at][:, TOK - 1 :] - shifts[at]).T
        ended = dot(b_ref[...], landed[:, lane_block(at, LANES)])
        for pair in range(GROUP // 2):
            here = slice(pair * HALF, (pair + 1) * HALF)
            value = mixed[at, :, here] + ended[:, here] * jnp.exp(pair_cols(last, pair))
            xbuf[slot, :, here] = value.astype(BF16)
        store_group(at, slot).start()

    pair_copy.wait_recv()

    def add_pair(i, carry):
        zsend[i] = (chunks[core, i].astype(F32) + paired[i].astype(F32)).astype(BF16)
        return carry

    lax.fori_loop(0, RING, add_pair, 0)
    z_others(lambda to: z_copy(to, z).start())
    for turn, shift in enumerate((0, 1, 3, 2)):
        quarter = lax.rem(y + shift, SIDE)

        def wait_back(row, carry):
            k = SIDE * row + quarter

            @pl.when(k != me)
            def _():
                back_copy(me, k).wait_recv()

            return carry

        lax.fori_loop(0, SIDE, wait_back, 0)
        for i in range(2):
            combine(2 * quarter + i, 2 * turn + i)
    z_others(lambda k: z_copy(k, k).wait_recv())
    zrecv[z] = zsend[z]
    summed = zrecv[0].astype(F32)
    for k in range(1, RING):
        summed += zrecv[k].astype(F32)
    grad_ref[...] = summed[:, :OWN]

    store_group(0, 0).wait()
    store_group(0, 1).wait()

    def finish(to):
        fac_copy(to, me).wait_send()
        push_copy(to, to, me).wait_send()
        square_copy(to, me).wait_send()
        back_copy(to, me).wait_send()

    others(finish)
    pair_copy.wait_send()
    z_others(lambda to: z_copy(to, z).wait_send())
    each_thin_out(lambda i: thin_send(i).wait_send())
    for s in (1, 3):
        o_copy(s, a).wait_send()
        g_copy(s, a).wait_send()
    for half in range(2):
        o_relay(half, left if half == 0 else right).wait_send()
        g_far(half).wait_send()
        g_relay(half, left if half == 0 else right).wait_send()
        y_far(half).wait_send()
        for side in range(2):
            y_near(side, half).wait_send()
    for turn in range(4):
        for half in range(2):
            for way in range(2):
                if turn == 3 and half != way:
                    continue
                at = lax.rem(z + (RING - turn if way == 0 else turn), RING)
                ring_copy(way, turn, half, at).wait_send()

    def finish_sib(at, carry):
        for part in range(SIDE):
            sib_copy(at, core, part).wait_send()
        return carry

    lax.fori_loop(0, RING, finish_sib, 0)

    def finish_side(at):
        for half in range(2):
            side_copy(at, half, odd).wait_send()

    z_others(finish_side)
    finish_side(z)


def layer(scale, *operands):
    vmem = pl.BlockSpec(memory_space=pltpu.VMEM)
    hbm = pl.BlockSpec(memory_space=pl.ANY)
    dma = pltpu.SemaphoreType.DMA
    ram = pltpu.VMEM
    return pl.pallas_call(
        functools.partial(layer_kernel, scale),
        out_shape=(jax.ShapeDtypeStruct((TOK, INNER), BF16), jax.ShapeDtypeStruct((COLS, OWN), F32)),
        in_specs=[hbm, hbm, vmem, vmem, hbm] + [vmem] * 5,
        out_specs=(hbm, vmem),
        scratch_shapes=[
            ram((GROUPS, 16, TOK), F32),
            ram((GROUPS, 16, HALF), F32),
            ram((GROUPS, 16, TOK), F32),
            ram((GROUPS, 16, TOK), F32),
            ram((2, TOK, LANES), BF16),
            ram((2, LANES, STATE), BF16),
            ram((TOK, INNER), BF16),
            ram((GROUPS, TOK, LANES), F32),
            ram((GROUPS, TOK, LANES), BF16),
            ram((TOK, TOK), F32),
            ram((TOK, TOK), F32),
            ram((TOK, HALF), F32),
            ram((TOK, HALF), F32),
            ram((INNER, TOK), BF16),
            ram((16, MODEL + WIDE), BF16),
            ram((RING, 16, MODEL + WIDE), BF16),
            ram((RING, 2 * OWN, MODEL), BF16),
            ram((SIDE, MODEL, TOK), BF16),
            ram((SIDE, TOK, MODEL), BF16),
            ram((SIDE, OWN, MODEL), BF16),
            ram((2, OWN, MODEL), BF16),
            ram((2, MODEL // 2, TOK), BF16),
            ram((2, OWN // 2, MODEL), BF16),
            ram((WIDE, MODEL), F32),
            ram((8, HALF), F32),
            ram((CTX, 8, HALF), F32),
            ram((2, RING, COLS, WIDE), BF16),
            ram((RING, COLS, WIDE), BF16),
            ram((RING, COLS, WIDE), BF16),
            ram((RING, COLS, WIDE), BF16),
            ram((8, HALF), F32),
            ram((CTX, 8, HALF), F32),
            ram((HALF, LANES), F32),
            ram((STATE, TOK), BF16),
            ram((STATE, INNER), BF16),
            ram((CTX, THIN, MODEL), BF16),
            ram((THIN, MODEL), F32),
            ram((CTX, THIN, MODEL), BF16),
            ram((STATE, INNER), BF16),
        ]
        + [dma((GROUPS,))]
        + [dma((2,))] * 3
        + [dma((RING,))] * 2
        + [dma((16,))] * 2
        + [dma((RING, 2))] * 2
        + [dma((RING, SIDE))] * 2
        + [dma((SIDE,))] * 6
        + [dma((2,))] * 4
        + [dma((CTX,))] * 2
        + [dma, dma]
        + [dma((RING,))] * 2
        + [dma((CTX,))] * 6,
        compiler_params=pltpu.CompilerParams(
            collective_id=0, has_side_effects=True, vmem_limit_bytes=VMEM_BYTES
        ),
        cost_estimate=pl.CostEstimate(flops=14 * 10**9, bytes_accessed=100 * 10**6, transcendentals=3 * 10**7),
        name="layer",
    )(*operands)


def per_device(
    ssm_input,
    gate_input,
    input_map,
    output_map,
    step_size,
    log_rate,
    entry_state,
    norm_gain,
    out_weight,
    out_grad,
):
    scale = math.sqrt(INNER * MODEL / lax.axis_size("dp"))
    input_grad, summed = layer(
        scale,
        ssm_input[0],
        gate_input[0],
        step_size[0],
        log_rate.reshape(1, HEADS),
        entry_state.reshape(INNER, STATE),
        input_map[0],
        output_map[0],
        norm_gain.reshape(1, INNER),
        out_weight,
        out_grad[0],
    )
    return (input_grad[None], summed.T)


def solution(mesh):
    placed = (
        P("dp", "ctx", None),
        P("dp", "ctx", None),
        P("dp", "ctx", None),
        P("dp", "ctx", None),
        P("dp", None, "ctx"),
        P(),
        P("dp", "ctx", None, None, None),
        P(),
        P(("dp", "ctx"), None),
        P("dp", "ctx", None),
    )
    return jax.shard_map(
        per_device,
        mesh=mesh,
        in_specs=placed,
        out_specs=(P("dp", "ctx", None), P("ctx", "dp")),
        check_vma=False,
    )
```

```python
import functools
import math

import jax
import jax.numpy as jnp
from jax import lax
from jax.experimental import pallas as pl
from jax.experimental.pallas import tpu as pltpu
from jax.sharding import PartitionSpec as P

NORM_EPS = 1e-05
CLIP_EPS = 1e-06
MESH = pl.DeviceIdType.MESH
F32 = jnp.float32
BF16 = jnp.bfloat16
HIGHEST = lax.Precision.HIGHEST

TOK = 256
HALF = 128
STATE = 128
HEADS = 80
GROUP = 10
LANES = 640
GROUPS = 8
INNER = 5120
MODEL = 1280
CAP = 80.0
SIDE = 4
CTX = 16
RING = 8
OWN = INNER // CTX
WIDE = 384
COLS = MODEL // 16
THIN = 32
EARLY = 3
THINAT = 6
VMEM_BYTES = 60 * 1024 * 1024


def dot(a, b):
    return jnp.dot(a, b, preferred_element_type=F32)


def dot_nt(a, b):
    return lax.dot_general(a, b, (((1,), (1,)), ((), ())), preferred_element_type=F32)


def rows_of(shape):
    return lax.broadcasted_iota(jnp.int32, shape, 0)


def lanes_of(shape):
    return lax.broadcasted_iota(jnp.int32, shape, 1)


def low_half():
    return lanes_of((TOK, HALF)) < HALF // 2


def pair_cols(columns, pair):
    return jnp.where(low_half(), columns[:, 2 * pair : 2 * pair + 1], columns[:, 2 * pair + 1 : 2 * pair + 2])


def split_pair(values):
    zero = jnp.zeros_like(values)
    return jnp.where(low_half(), values, zero), jnp.where(low_half(), zero, values)


def silu(gate):
    return gate / (1.0 + jnp.exp(-gate))


def lane_block(at, width):
    return pl.ds(pl.multiple_of(at * width, HALF), width)


def layer_kernel(
    scale,
    x_ref,
    z_hbm,
    st_ref,
    lr_ref,
    s_ref,
    b_ref,
    c_ref,
    gain_ref,
    w_ref,
    og_ref,
    out_ref,
    grad_ref,
    steps,
    rates,
    cums,
    shifts,
    xbuf,
    sbuf,
    z_ref,
    mixed,
    gated,
    coup,
    upper,
    acc,
    rms,
    turned,
    wpad,
    thin,
    full,
    gx,
    ox,
    partial,
    landing,
    relay,
    ybuf,
    term,
    square_own,
    squares,
    chunks,
    paired,
    zsend,
    zrecv,
    fac,
    facs,
    expanded,
    ct,
    pushed,
    arrived,
    running,
    back,
    landed,
    gate_sem,
    x_sem,
    s_sem,
    out_sem,
    w_send,
    w_recv,
    ring_send,
    ring_recv,
    wy_send,
    wy_recv,
    sib_send,
    sib_recv,
    o_send,
    o_recv,
    g_send,
    g_recv,
    y_send,
    y_recv,
    r_send,
    r_recv,
    yf_send,
    yf_recv,
    q_send,
    q_recv,
    pair_send,
    pair_recv,
    z_send,
    z_recv,
    f_send,
    f_recv,
    p_send,
    p_recv,
    b_send,
    b_recv,
):
    dp, me = lax.axis_index("dp"), lax.axis_index("ctx")
    core, z = lax.rem(dp, 2), lax.div(dp, 2)
    x, y = lax.div(me, SIDE), lax.rem(me, SIDE)
    partner = dp + 1 - 2 * core
    first = core == 0
    a, r = jnp.where(first, x, y), jnp.where(first, y, x)

    def over_x(s):
        return lax.rem(x + s, SIDE) * SIDE + y

    def over_y(s):
        return x * SIDE + lax.rem(y + s, SIDE)

    def a_peer(s):
        return (dp, jnp.where(first, over_x(s), over_y(s)))

    def r_peer(s):
        return (dp, jnp.where(first, over_y(s), over_x(s)))

    def remote(src, dst, send, recv, to):
        return pltpu.make_async_remote_copy(
            src_ref=src, dst_ref=dst, send_sem=send, recv_sem=recv, device_id=to, device_id_type=MESH
        )

    def others(body):
        def turn(s, carry):
            body(lax.rem(me + s, CTX))
            return carry

        lax.fori_loop(1, CTX, turn, 0)

    def z_others(body):
        def turn(s, carry):
            body(lax.rem(z + s, RING))
            return carry

        lax.fori_loop(1, RING, turn, 0)

    def load_group(at):
        slot = lax.rem(at, 2)
        return (
            pltpu.make_async_copy(x_ref.at[:, lane_block(at, LANES)], xbuf.at[slot], x_sem.at[slot]),
            pltpu.make_async_copy(s_ref.at[lane_block(at, LANES)], sbuf.at[slot], s_sem.at[slot]),
        )

    def store_group(at, slot):
        return pltpu.make_async_copy(xbuf.at[slot], out_ref.at[:, lane_block(at, LANES)], out_sem.at[slot])

    def load_gate(at):
        lanes = lane_block(at, LANES)
        return pltpu.make_async_copy(z_hbm.at[:, lanes], z_ref.at[:, lanes], gate_sem.at[at])

    for copy in load_group(0):
        copy.start()
    for at in range(GROUPS):
        load_gate(at).start()

    barrier = pltpu.get_barrier_semaphore()

    def greet(to):
        pl.semaphore_signal(barrier, inc=1, device_id=(dp, to), device_id_type=MESH)

    def greet_z(to):
        pl.semaphore_signal(barrier, inc=1, device_id=(2 * to + core, me), device_id_type=MESH)

    others(greet)
    z_others(greet_z)
    pl.semaphore_signal(barrier, inc=1, device_id=(partner, me), device_id_type=MESH)

    weights = w_ref[...].astype(F32)
    wpad[:, :MODEL] = weights[:16].astype(BF16)
    rest = [weights[16:, WIDE * i : min(WIDE * (i + 1), MODEL)] for i in range(SIDE)]
    rest[-1] = jnp.concatenate([rest[-1], jnp.zeros((4, WIDE - rest[-1].shape[1]), F32)], axis=1)
    wpad[:, MODEL:] = jnp.concatenate(rest, axis=0).astype(BF16)

    odd = lax.rem(r, 2)
    part_of = lax.div(me, RING)

    def thin_from(i):
        return remote(wpad, thin.at[i], w_send.at[i], w_recv.at[i], (dp, RING * odd + i))

    def thin_out(i):
        along, across = 2 * lax.rem(i, 2) + part_of, lax.div(i, 2)
        return jnp.where(first, SIDE * across + along, SIDE * along + across)

    def thin_send(i):
        to = thin_out(i)
        return remote(wpad, thin.at[lax.rem(me, RING)], w_send.at[i], w_recv.at[lax.rem(me, RING)], (dp, to))

    def each_thin_out(body):
        def turn(i, carry):
            @pl.when(thin_out(i) != me)
            def _():
                body(i)

            return carry

        lax.fori_loop(0, RING, turn, 0)

    def block_part(at, which, part):
        row = pl.multiple_of(which * OWN + part * COLS, 16)
        return full.at[at, pl.ds(row, COLS)]

    def ring_copy(way, turn, half, at):
        slot = (way * 4 + turn) * 2 + half
        to = 2 * lax.rem(z + (1 if way == 0 else RING - 1), RING) + core
        block = block_part(at, core, 2 * odd + half)
        return remote(block, block, ring_send.at[slot], ring_recv.at[slot], (to, me))

    def side_copy(at, half, parity):
        block = block_part(at, core, 2 * parity + half)
        to = r_peer(1 if half == 0 else 3)
        return remote(block, block, wy_send.at[at, half], wy_recv.at[at, half], to)

    def sib_copy(at, which, part):
        block = block_part(at, which, part)
        return remote(block, block, sib_send.at[at, part], sib_recv.at[at, part], (partner, me))

    def o_copy(s, slot):
        return remote(og_ref, ox.at[slot], o_send.at[s], o_recv.at[s], a_peer(s))

    def o_relay(half, slot):
        block = ox.at[slot, pl.ds(half * HALF, HALF)]
        return remote(block, block, o_send.at[2 * half], o_recv.at[2 * half], a_peer(1 if half == 0 else 3))

    def turned_rows(s, half, count):
        to = lax.rem(a + s, SIDE)
        return turned.at[pl.ds(pl.multiple_of(to * MODEL + half * (MODEL // 2), HALF), count)]

    def g_copy(s, slot):
        return remote(turned_rows(s, 0, MODEL), gx.at[slot], g_send.at[s], g_recv.at[s], a_peer(s))

    def g_far(half):
        to = a_peer(1 if half == 0 else 3)
        return remote(turned_rows(2, half, MODEL // 2), relay.at[half], r_send.at[half], r_recv.at[half], to)

    def g_relay(half, slot):
        block = gx.at[slot, pl.ds(half * (MODEL // 2), MODEL // 2)]
        return remote(relay.at[half], block, g_send.at[2 * half], g_recv.at[2 * half], a_peer(1 if half == 0 else 3))

    def y_far(half):
        block = partial.at[2, pl.ds(half * (OWN // 2), OWN // 2)]
        return remote(block, ybuf.at[half], yf_send.at[half], yf_recv.at[half], r_peer(1 if half == 0 else 3))

    def y_near(side, half):
        rows = pl.ds(half * (OWN // 2), OWN // 2)
        s, slot = 1 + 2 * side, 2 * side + half
        return remote(partial.at[s, rows], landing.at[side, rows], y_send.at[slot], y_recv.at[slot], r_peer(s))

    def square_copy(to, slot):
        return remote(square_own, squares.at[slot], q_send.at[to], q_recv.at[slot], (dp, to))

    pair_copy = remote(chunks.at[1 - core], paired, pair_send, pair_recv, (partner, me))

    def z_copy(to, slot):
        return remote(zsend.at[to], zrecv.at[slot], z_send.at[to], z_recv.at[slot], (2 * to + core, me))

    def piece(ref, owner):
        row = pl.multiple_of(lax.div(owner, SIDE) * THIN, THIN)
        return ref.at[pl.ds(row, THIN), lane_block(lax.rem(owner, SIDE), MODEL)]

    def fac_copy(to, slot):
        return remote(fac, facs.at[slot], f_send.at[to], f_recv.at[slot], (dp, to))

    def push_copy(src, to, slot):
        return remote(piece(pushed, src), arrived.at[slot], p_send.at[to], p_recv.at[slot], (dp, to))

    def back_copy(to, owner):
        return remote(back.at[to], piece(landed, owner), b_send.at[to], b_recv.at[owner], (dp, to))


    for at in range(GROUPS):
        steps[at, :GROUP, :] = st_ref[at * GROUP : (at + 1) * GROUP, :]
    rate_rows = jnp.broadcast_to(jnp.exp(lr_ref[...]), (HALF, HEADS)).T
    for at in range(GROUPS):
        rates[at, :GROUP, :] = rate_rows[at * GROUP : (at + 1) * GROUP, :]
    square = (TOK, TOK)
    coup[...] = jnp.where(rows_of(square) >= lanes_of(square), dot_nt(c_ref[...], b_ref[...]), 0.0)
    upper[...] = jnp.where(rows_of(square) <= lanes_of(square), 1.0, 0.0).astype(F32)
    ct[...] = c_ref[...].astype(F32).T.astype(BF16)
    acc[...] = jnp.zeros_like(acc)
    fac[...] = jnp.zeros_like(fac)

    def forward(at, carry):
        slot = lax.rem(at, 2)

        @pl.when(at + 1 < GROUPS)
        def _():
            for copy in load_group(at + 1):
                copy.start()

        step = steps[at, :GROUP, :]
        drop = -(rates[at, :GROUP, :1] * step)
        cumulative = jnp.dot(drop, upper[...], preferred_element_type=F32, precision=HIGHEST)
        shifted = cumulative - jnp.log(step)
        cums[at, :GROUP, :] = cumulative
        shifts[at, :GROUP, :] = shifted
        columns = cumulative.T
        fac[pl.ds(at, 1), :GROUP] = jnp.exp(columns[TOK - 1 :, :])
        for copy in load_group(at):
            copy.wait()
        load_gate(at).wait()
        for pair in range(GROUP // 2):
            here = slice(pair * HALF, (pair + 1) * HALF)
            parts = split_pair(xbuf[slot, :, here])
            top = bottom = None
            for which in range(2):
                head = 2 * pair + which
                col = columns[:, head : head + 1]
                row = shifted[head : head + 1, :]
                m_top = jnp.exp(jnp.minimum(col[:HALF] - row[:, :HALF], CAP)) * coup[:HALF, :HALF]
                m_bot = jnp.exp(jnp.minimum(col[HALF:] - row, CAP)) * coup[HALF:, :]
                t = dot(m_top.astype(BF16), parts[which][:HALF])
                b = dot(m_bot.astype(BF16), parts[which])
                top = t if top is None else top + t
                bottom = b if bottom is None else bottom + b
            inside = jnp.concatenate([top, bottom], axis=0)
            carried = dot_nt(c_ref[...], sbuf[slot, here, :])
            value = inside + carried * jnp.exp(pair_cols(columns, pair))
            lanes = pl.ds(pl.multiple_of(at * LANES + pair * HALF, HALF), HALF)
            mix = value * silu(z_ref[:, lanes].astype(F32))
            mixed[at, :, here] = mix
            acc[...] += mix * mix
        return carry

    def arriving(turn, half):
        for way in (0, 1):
            if turn < 3 or half == way:
                yield way, lax.rem(z + (RING - turn - 1 if way == 0 else turn + 1), RING)

    def arrive(turn, half):
        for way, at in arriving(turn, half):
            ring_copy(way, turn, half, at).wait_recv()
            if turn < 2 or (turn == 2 and half == way):
                ring_copy(way, turn + 1, half, at).start()
            side_copy(at, half, odd).start()
            sib_copy(at, core, 2 * odd + half).start()

    def arrive_side(turn, half):
        for _, at in arriving(turn, half):
            side_copy(at, half, 1 - odd).wait_recv()
            sib_copy(at, core, 2 * (1 - odd) + half).start()

    lax.fori_loop(0, EARLY, forward, 0)
    pl.semaphore_wait(barrier, CTX - 1 + RING - 1 + 1)
    def push_to(to):
        @pl.when(to != me)
        def _():
            push_copy(to, to, me).start()

    each_thin_out(lambda i: thin_send(i).start())
    lax.fori_loop(EARLY, THINAT, forward, 0)

    def wait_thin(i, carry):
        k = RING * odd + i

        @pl.when(k != me)
        def _():
            thin_from(i).wait_recv()

        return carry

    @pl.when(part_of == odd)
    def _():
        thin[lax.rem(me, RING)] = wpad[...]

    lax.fori_loop(0, RING, wait_thin, 0)
    rows = []
    for k in range(RING):
        value = thin[k].astype(F32)
        rest = [value[4 * i : 4 * i + 4, MODEL:] for i in range(SIDE)]
        rows += [value[:, :MODEL], jnp.concatenate(rest, axis=1)[:, :MODEL]]
    half_rows = pl.ds(pl.multiple_of(core * OWN + odd * (OWN // 2), 16), OWN // 2)
    full[z, half_rows] = jnp.concatenate(rows, axis=0).astype(BF16)
    for half in range(2):
        for way in range(2):
            ring_copy(way, 0, half, z).start()
        side_copy(z, half, odd).start()
        sib_copy(z, core, 2 * odd + half).start()
    for s in (1, 3):
        o_copy(s, a).start()
    lax.fori_loop(THINAT, GROUPS, forward, 0)

    inverse = lax.rsqrt(jnp.sum(acc[...], axis=1, keepdims=True) * (1.0 / INNER) + NORM_EPS)
    rms[...] = jnp.broadcast_to(inverse, rms.shape)

    def finish_norm(at, carry):
        lanes = lane_block(at, LANES)
        normed = mixed[at] * rms[:, :1] * gain_ref[:, lanes]
        gated[at] = normed.astype(BF16)
        rows = normed.T.astype(BF16)
        for which in range(2):
            block = 2 * at + which
            place = jnp.where(first, block, SIDE * lax.rem(block, SIDE) + lax.div(block, SIDE))
            turned[pl.ds(pl.multiple_of(place * OWN, OWN), OWN), :] = rows[which * OWN : (which + 1) * OWN]
        return carry

    lax.fori_loop(0, GROUPS, finish_norm, 0)

    for half in range(2):
        g_far(half).start()
    for s in (1, 3):
        g_copy(s, a).start()

    left, right = lax.rem(a + 3, SIDE), lax.rem(a + 1, SIDE)
    gx[a] = turned[pl.ds(pl.multiple_of(a * MODEL, MODEL), MODEL), :]
    ox[a] = og_ref[...]
    others(lambda to: fac_copy(to, me).start())
    acc[...] = jnp.zeros_like(acc)

    def product(at):
        for part in range(SIDE):
            sib_copy(at, 1 - core, part).wait_recv()
        value = dot_nt(og_ref[...], full[at])
        mixed[at] = value
        both = value * gated[at].astype(F32)
        total = acc[...]
        for i in range(LANES // HALF):
            total += both[:, i * HALF : (i + 1) * HALF]
        acc[...] = total

    def weight_part(s):
        rows = pl.ds(pl.multiple_of(lax.rem(r + s, SIDE) * OWN, OWN), OWN)
        total = None
        for source in range(SIDE):
            part = dot(gx[source, rows, :], ox[source])
            total = part if total is None else total + part
        partial[s] = total.astype(BF16)

    def near(step):
        return lax.rem(z + step, RING)

    arrive(0, 0)
    arrive(0, 1)
    o_copy(1, left).wait_recv()
    o_relay(0, left).start()
    o_copy(3, right).wait_recv()
    o_relay(1, right).start()
    for half in range(2):
        side_copy(z, half, 1 - odd).wait_recv()
        sib_copy(z, core, 2 * (1 - odd) + half).start()
    arrive(1, 0)
    arrive_side(0, 0)
    product(z)
    arrive(1, 1)
    arrive_side(0, 1)
    for half in range(2):
        g_far(half).wait_recv()
        g_relay(half, left if half == 0 else right).start()
    arrive(2, 0)
    arrive_side(1, 0)
    product(near(1))
    product(near(7))
    arrive(2, 1)
    arrive_side(1, 1)
    arrive(3, 0)
    arrive_side(2, 0)
    product(near(2))
    product(near(6))
    arrive(3, 1)
    arrive_side(2, 1)
    arrive_side(3, 0)
    product(near(3))
    product(near(5))
    arrive_side(3, 1)
    far = lax.rem(a + 2, SIDE)
    for half in range(2):
        o_relay(half, far).wait_recv()
        g_relay(half, far).wait_recv()
    g_copy(1, left).wait_recv()
    g_copy(3, right).wait_recv()
    weight_part(2)
    for half in range(2):
        y_far(half).start()
    weight_part(1)
    y_near(0, 1).start()
    weight_part(3)
    y_near(1, 0).start()
    product(near(4))
    weight_part(0)
    for half in range(2):
        y_far(half).wait_recv()
        at = slice(half * (OWN // 2), (half + 1) * (OWN // 2))
        added = partial[1 + 2 * half, at].astype(F32) + ybuf[half].astype(F32)
        partial[1 + 2 * half, at] = added.astype(BF16)
        y_near(half, half).start()
    mean = jnp.sum(acc[...], axis=1, keepdims=True) * (1.0 / INNER)
    acc[...] = jnp.broadcast_to(mean, acc.shape)

    def norm_back(at, carry):
        columns = cums[at].T
        for pair in range(GROUP // 2):
            here = slice(pair * HALF, (pair + 1) * HALF)
            lanes = pl.ds(pl.multiple_of(at * LANES + pair * HALF, HALF), HALF)
            gain = gain_ref[:, lanes]
            inner = gain * mixed[at, :, here] - gated[at, :, here].astype(F32) * (1.0 / gain) * acc[...]
            yg = silu(z_ref[:, lanes].astype(F32)) * rms[...] * inner
            gated[at, :, here] = yg.astype(BF16)
            weighted = (yg * jnp.exp(pair_cols(columns, pair))).astype(BF16)
            pushed[:, lanes] = dot(ct[...], weighted).astype(BF16)
        return carry

    for shift in (2, 1, 3, 0):
        quarter = lax.rem(y + shift, SIDE)
        lax.fori_loop(2 * quarter, 2 * quarter + 2, norm_back, 0)
        for row in range(SIDE):
            push_to(SIDE * lax.rem(x + (2, 1, 3, 0)[row], SIDE) + quarter)

    coup[...] = jnp.where(rows_of(square) <= lanes_of(square), dot_nt(b_ref[...], c_ref[...]), 0.0)

    def inside_back(at, carry):
        shifted = shifts[at]
        columns = shifted.T
        for pair in range(GROUP // 2):
            here = slice(pair * HALF, (pair + 1) * HALF)
            parts = split_pair(gated[at, :, here])
            top = bottom = None
            for which in range(2):
                head = 2 * pair + which
                col = columns[:, head : head + 1]
                row = cums[at, head : head + 1, :]
                m_top = jnp.exp(jnp.minimum(row - col[:HALF], CAP)) * coup[:HALF, :]
                m_bot = jnp.exp(jnp.minimum(row[:, HALF:] - col[HALF:], CAP)) * coup[HALF:, HALF:]
                t = dot(m_top.astype(BF16), parts[which])
                b = dot(m_bot.astype(BF16), parts[which][HALF:])
                top = t if top is None else top + t
                bottom = b if bottom is None else bottom + b
            mixed[at, :HALF, here] = top
            mixed[at, HALF:, here] = bottom
        return carry

    lax.fori_loop(0, 4, inside_back, 0)
    lax.fori_loop(4, GROUPS, inside_back, 0)
    for side in range(2):
        for half in range(2):
            y_near(side, half).wait_recv()
    total = partial[0].astype(F32)
    for side in range(2):
        total += landing[side].astype(F32)
    term[:OWN, :] = total
    term[OWN:, :] = jnp.zeros((WIDE - OWN, MODEL), F32)
    folded = jnp.sum((total * total).reshape(OWN // 8, 8, MODEL), axis=0)
    part = folded[:, :HALF]
    for i in range(1, MODEL // HALF):
        part += folded[:, i * HALF : (i + 1) * HALF]
    square_own[...] = part
    others(lambda to: square_copy(to, me).start())

    arrived[me] = piece(pushed, me)[...]
    facs[me] = fac[...]
    others(lambda k: fac_copy(k, k).wait_recv())
    shape = (HALF, LANES)
    hot = jnp.where(rows_of(shape) == lax.shift_right_logical(lanes_of(shape), 6), 1.0, 0.0).astype(F32)
    listed = jnp.concatenate([facs[k] for k in range(CTX)], axis=0)
    expanded[...] = jnp.dot(listed, hot, preferred_element_type=F32, precision=HIGHEST)
    running[...] = jnp.zeros_like(running)

    def chain(turn, carry):
        k = CTX - 1 - turn

        @pl.when(k != me)
        def _():
            push_copy(k, k, k).wait_recv()

        now = running[...]
        back[k] = now.astype(BF16)

        first = k * GROUPS + 2 * lax.rem(me, SIDE)
        factor = jnp.concatenate([expanded[pl.ds(first, 1), :], expanded[pl.ds(first + 1, 1), :]], axis=1)
        running[...] = factor * now + arrived[k].astype(F32)
        return carry

    lax.fori_loop(0, CTX, chain, 0)
    piece(landed, me)[...] = back[me]
    others(lambda to: back_copy(to, me).start())
    others(lambda k: square_copy(k, k).wait_recv())
    squares[me] = square_own[...]
    all_squares = squares[0]
    for k in range(1, CTX):
        all_squares += squares[k]
    whole = jnp.sum(jnp.sum(all_squares, axis=1, keepdims=True), axis=0, keepdims=True)
    clip = jnp.minimum(1.0, lax.rsqrt(whole + CLIP_EPS)) * scale
    for i in range(MODEL // HALF):
        block = (term[:, i * HALF : (i + 1) * HALF] * clip).T
        lo = i * HALF
        while lo < (i + 1) * HALF:
            owner = lo // COLS
            hi = min((i + 1) * HALF, (owner + 1) * COLS)
            at = slice(lo - owner * COLS, hi - owner * COLS)
            chunks[owner % 2, owner // 2, at] = block[lo - i * HALF : hi - i * HALF].astype(BF16)
            lo = hi
    pair_copy.start()

    def combine(at, count):
        slot = count % 2
        if count >= 2:
            store_group(at, slot).wait()
        last = (cums[at][:, TOK - 1 :] - shifts[at]).T
        ended = dot(b_ref[...], landed[:, lane_block(at, LANES)])
        for pair in range(GROUP // 2):
            here = slice(pair * HALF, (pair + 1) * HALF)
            value = mixed[at, :, here] + ended[:, here] * jnp.exp(pair_cols(last, pair))
            xbuf[slot, :, here] = value.astype(BF16)
        store_group(at, slot).start()

    pair_copy.wait_recv()

    def add_pair(i, carry):
        zsend[i] = (chunks[core, i].astype(F32) + paired[i].astype(F32)).astype(BF16)
        return carry

    lax.fori_loop(0, RING, add_pair, 0)
    z_others(lambda to: z_copy(to, z).start())
    for turn, shift in enumerate((0, 1, 3, 2)):
        quarter = lax.rem(y + shift, SIDE)

        def wait_back(row, carry):
            k = SIDE * row + quarter

            @pl.when(k != me)
            def _():
                back_copy(me, k).wait_recv()

            return carry

        lax.fori_loop(0, SIDE, wait_back, 0)
        for i in range(2):
            combine(2 * quarter + i, 2 * turn + i)
    z_others(lambda k: z_copy(k, k).wait_recv())
    zrecv[z] = zsend[z]
    summed = zrecv[0].astype(F32)
    for k in range(1, RING):
        summed += zrecv[k].astype(F32)
    grad_ref[...] = summed[:, :OWN]

    store_group(0, 0).wait()
    store_group(0, 1).wait()

    def finish(to):
        fac_copy(to, me).wait_send()
        push_copy(to, to, me).wait_send()
        square_copy(to, me).wait_send()
        back_copy(to, me).wait_send()

    others(finish)
    pair_copy.wait_send()
    z_others(lambda to: z_copy(to, z).wait_send())
    each_thin_out(lambda i: thin_send(i).wait_send())
    for s in (1, 3):
        o_copy(s, a).wait_send()
        g_copy(s, a).wait_send()
    for half in range(2):
        o_relay(half, left if half == 0 else right).wait_send()
        g_far(half).wait_send()
        g_relay(half, left if half == 0 else right).wait_send()
        y_far(half).wait_send()
        for side in range(2):
            y_near(side, half).wait_send()
    for turn in range(4):
        for half in range(2):
            for way in range(2):
                if turn == 3 and half != way:
                    continue
                at = lax.rem(z + (RING - turn if way == 0 else turn), RING)
                ring_copy(way, turn, half, at).wait_send()

    def finish_sib(at, carry):
        for part in range(SIDE):
            sib_copy(at, core, part).wait_send()
        return carry

    lax.fori_loop(0, RING, finish_sib, 0)

    def finish_side(at):
        for half in range(2):
            side_copy(at, half, odd).wait_send()

    z_others(finish_side)
    finish_side(z)


def layer(scale, *operands):
    vmem = pl.BlockSpec(memory_space=pltpu.VMEM)
    hbm = pl.BlockSpec(memory_space=pl.ANY)
    dma = pltpu.SemaphoreType.DMA
    ram = pltpu.VMEM
    return pl.pallas_call(
        functools.partial(layer_kernel, scale),
        out_shape=(jax.ShapeDtypeStruct((TOK, INNER), BF16), jax.ShapeDtypeStruct((COLS, OWN), F32)),
        in_specs=[hbm, hbm, vmem, vmem, hbm] + [vmem] * 5,
        out_specs=(hbm, vmem),
        scratch_shapes=[
            ram((GROUPS, 16, TOK), F32),
            ram((GROUPS, 16, HALF), F32),
            ram((GROUPS, 16, TOK), F32),
            ram((GROUPS, 16, TOK), F32),
            ram((2, TOK, LANES), BF16),
            ram((2, LANES, STATE), BF16),
            ram((TOK, INNER), BF16),
            ram((GROUPS, TOK, LANES), F32),
            ram((GROUPS, TOK, LANES), BF16),
            ram((TOK, TOK), F32),
            ram((TOK, TOK), F32),
            ram((TOK, HALF), F32),
            ram((TOK, HALF), F32),
            ram((INNER, TOK), BF16),
            ram((16, MODEL + WIDE), BF16),
            ram((RING, 16, MODEL + WIDE), BF16),
            ram((RING, 2 * OWN, MODEL), BF16),
            ram((SIDE, MODEL, TOK), BF16),
            ram((SIDE, TOK, MODEL), BF16),
            ram((SIDE, OWN, MODEL), BF16),
            ram((2, OWN, MODEL), BF16),
            ram((2, MODEL // 2, TOK), BF16),
            ram((2, OWN // 2, MODEL), BF16),
            ram((WIDE, MODEL), F32),
            ram((8, HALF), F32),
            ram((CTX, 8, HALF), F32),
            ram((2, RING, COLS, WIDE), BF16),
            ram((RING, COLS, WIDE), BF16),
            ram((RING, COLS, WIDE), BF16),
            ram((RING, COLS, WIDE), BF16),
            ram((8, HALF), F32),
            ram((CTX, 8, HALF), F32),
            ram((HALF, LANES), F32),
            ram((STATE, TOK), BF16),
            ram((STATE, INNER), BF16),
            ram((CTX, THIN, MODEL), BF16),
            ram((THIN, MODEL), F32),
            ram((CTX, THIN, MODEL), BF16),
            ram((STATE, INNER), BF16),
        ]
        + [dma((GROUPS,))]
        + [dma((2,))] * 3
        + [dma((RING,))] * 2
        + [dma((16,))] * 2
        + [dma((RING, 2))] * 2
        + [dma((RING, SIDE))] * 2
        + [dma((SIDE,))] * 6
        + [dma((2,))] * 4
        + [dma((CTX,))] * 2
        + [dma, dma]
        + [dma((RING,))] * 2
        + [dma((CTX,))] * 6,
        compiler_params=pltpu.CompilerParams(
            collective_id=0, has_side_effects=True, vmem_limit_bytes=VMEM_BYTES
        ),
        cost_estimate=pl.CostEstimate(flops=14 * 10**9, bytes_accessed=100 * 10**6, transcendentals=3 * 10**7),
        name="layer",
    )(*operands)


def per_device(
    ssm_input,
    gate_input,
    input_map,
    output_map,
    step_size,
    log_rate,
    entry_state,
    norm_gain,
    out_weight,
    out_grad,
):
    scale = math.sqrt(INNER * MODEL / lax.axis_size("dp"))
    input_grad, summed = layer(
        scale,
        ssm_input[0],
        gate_input[0],
        step_size[0],
        log_rate.reshape(1, HEADS),
        entry_state.reshape(INNER, STATE),
        input_map[0],
        output_map[0],
        norm_gain.reshape(1, INNER),
        out_weight,
        out_grad[0],
    )
    return (input_grad[None], summed.T)


def solution(mesh):
    placed = (
        P("dp", "ctx", None),
        P("dp", "ctx", None),
        P("dp", "ctx", None),
        P("dp", "ctx", None),
        P("dp", None, "ctx"),
        P(),
        P("dp", "ctx", None, None, None),
        P(),
        P(("dp", "ctx"), None),
        P("dp", "ctx", None),
    )
    return jax.shard_map(
        per_device,
        mesh=mesh,
        in_specs=placed,
        out_specs=(P("dp", "ctx", None), P("ctx", "dp")),
        check_vma=False,
    )
```

```python
import functools
import math

import jax
import jax.numpy as jnp
from jax import lax
from jax.experimental import pallas as pl
from jax.experimental.pallas import tpu as pltpu
from jax.sharding import PartitionSpec as P

NORM_EPS = 1e-05
CLIP_EPS = 1e-06
MESH = pl.DeviceIdType.MESH
F32 = jnp.float32
BF16 = jnp.bfloat16
HIGHEST = lax.Precision.HIGHEST

TOK = 256
HALF = 128
STATE = 128
HEADS = 80
GROUP = 10
LANES = 640
GROUPS = 8
INNER = 5120
MODEL = 1280
CAP = 80.0
SIDE = 4
CTX = 16
RING = 8
OWN = INNER // CTX
WIDE = 384
COLS = MODEL // 16
THIN = 32
EARLY = 3
THINAT = 7
VMEM_BYTES = 60 * 1024 * 1024


def dot(a, b):
    return jnp.dot(a, b, preferred_element_type=F32)


def dot_nt(a, b):
    return lax.dot_general(a, b, (((1,), (1,)), ((), ())), preferred_element_type=F32)


def rows_of(shape):
    return lax.broadcasted_iota(jnp.int32, shape, 0)


def lanes_of(shape):
    return lax.broadcasted_iota(jnp.int32, shape, 1)


def low_half():
    return lanes_of((TOK, HALF)) < HALF // 2


def pair_cols(columns, pair):
    return jnp.where(low_half(), columns[:, 2 * pair : 2 * pair + 1], columns[:, 2 * pair + 1 : 2 * pair + 2])


def split_pair(values):
    zero = jnp.zeros_like(values)
    return jnp.where(low_half(), values, zero), jnp.where(low_half(), zero, values)


def silu(gate):
    return gate / (1.0 + jnp.exp(-gate))


def lane_block(at, width):
    return pl.ds(pl.multiple_of(at * width, HALF), width)


def layer_kernel(
    scale,
    x_ref,
    z_hbm,
    st_ref,
    lr_ref,
    s_ref,
    b_ref,
    c_ref,
    gain_ref,
    w_ref,
    og_ref,
    out_ref,
    grad_ref,
    steps,
    rates,
    cums,
    shifts,
    xbuf,
    sbuf,
    z_ref,
    mixed,
    gated,
    coup,
    upper,
    acc,
    rms,
    turned,
    wpad,
    thin,
    full,
    gx,
    ox,
    partial,
    landing,
    relay,
    ybuf,
    term,
    square_own,
    squares,
    chunks,
    paired,
    zsend,
    zrecv,
    fac,
    facs,
    expanded,
    ct,
    pushed,
    arrived,
    running,
    back,
    landed,
    gate_sem,
    x_sem,
    s_sem,
    out_sem,
    w_send,
    w_recv,
    ring_send,
    ring_recv,
    wy_send,
    wy_recv,
    sib_send,
    sib_recv,
    o_send,
    o_recv,
    g_send,
    g_recv,
    y_send,
    y_recv,
    r_send,
    r_recv,
    yf_send,
    yf_recv,
    q_send,
    q_recv,
    pair_send,
    pair_recv,
    z_send,
    z_recv,
    f_send,
    f_recv,
    p_send,
    p_recv,
    b_send,
    b_recv,
):
    dp, me = lax.axis_index("dp"), lax.axis_index("ctx")
    core, z = lax.rem(dp, 2), lax.div(dp, 2)
    x, y = lax.div(me, SIDE), lax.rem(me, SIDE)
    partner = dp + 1 - 2 * core
    first = core == 0
    a, r = jnp.where(first, x, y), jnp.where(first, y, x)

    def over_x(s):
        return lax.rem(x + s, SIDE) * SIDE + y

    def over_y(s):
        return x * SIDE + lax.rem(y + s, SIDE)

    def a_peer(s):
        return (dp, jnp.where(first, over_x(s), over_y(s)))

    def r_peer(s):
        return (dp, jnp.where(first, over_y(s), over_x(s)))

    def remote(src, dst, send, recv, to):
        return pltpu.make_async_remote_copy(
            src_ref=src, dst_ref=dst, send_sem=send, recv_sem=recv, device_id=to, device_id_type=MESH
        )

    def others(body):
        def turn(s, carry):
            body(lax.rem(me + s, CTX))
            return carry

        lax.fori_loop(1, CTX, turn, 0)

    def z_others(body):
        def turn(s, carry):
            body(lax.rem(z + s, RING))
            return carry

        lax.fori_loop(1, RING, turn, 0)

    def load_group(at):
        slot = lax.rem(at, 2)
        return (
            pltpu.make_async_copy(x_ref.at[:, lane_block(at, LANES)], xbuf.at[slot], x_sem.at[slot]),
            pltpu.make_async_copy(s_ref.at[lane_block(at, LANES)], sbuf.at[slot], s_sem.at[slot]),
        )

    def store_group(at, slot):
        return pltpu.make_async_copy(xbuf.at[slot], out_ref.at[:, lane_block(at, LANES)], out_sem.at[slot])

    def load_gate(at):
        lanes = lane_block(at, LANES)
        return pltpu.make_async_copy(z_hbm.at[:, lanes], z_ref.at[:, lanes], gate_sem.at[at])

    for copy in load_group(0):
        copy.start()
    for at in range(GROUPS):
        load_gate(at).start()

    barrier = pltpu.get_barrier_semaphore()

    def greet(to):
        pl.semaphore_signal(barrier, inc=1, device_id=(dp, to), device_id_type=MESH)

    def greet_z(to):
        pl.semaphore_signal(barrier, inc=1, device_id=(2 * to + core, me), device_id_type=MESH)

    others(greet)
    z_others(greet_z)
    pl.semaphore_signal(barrier, inc=1, device_id=(partner, me), device_id_type=MESH)

    weights = w_ref[...].astype(F32)
    wpad[:, :MODEL] = weights[:16].astype(BF16)
    rest = [weights[16:, WIDE * i : min(WIDE * (i + 1), MODEL)] for i in range(SIDE)]
    rest[-1] = jnp.concatenate([rest[-1], jnp.zeros((4, WIDE - rest[-1].shape[1]), F32)], axis=1)
    wpad[:, MODEL:] = jnp.concatenate(rest, axis=0).astype(BF16)

    odd = lax.rem(r, 2)
    part_of = lax.div(me, RING)

    def thin_from(i):
        return remote(wpad, thin.at[i], w_send.at[i], w_recv.at[i], (dp, RING * odd + i))

    def thin_out(i):
        along, across = 2 * lax.rem(i, 2) + part_of, lax.div(i, 2)
        return jnp.where(first, SIDE * across + along, SIDE * along + across)

    def thin_send(i):
        to = thin_out(i)
        return remote(wpad, thin.at[lax.rem(me, RING)], w_send.at[i], w_recv.at[lax.rem(me, RING)], (dp, to))

    def each_thin_out(body):
        def turn(i, carry):
            @pl.when(thin_out(i) != me)
            def _():
                body(i)

            return carry

        lax.fori_loop(0, RING, turn, 0)

    def block_part(at, which, part):
        row = pl.multiple_of(which * OWN + part * COLS, 16)
        return full.at[at, pl.ds(row, COLS)]

    def ring_copy(way, turn, half, at):
        slot = (way * 4 + turn) * 2 + half
        to = 2 * lax.rem(z + (1 if way == 0 else RING - 1), RING) + core
        block = block_part(at, core, 2 * odd + half)
        return remote(block, block, ring_send.at[slot], ring_recv.at[slot], (to, me))

    def side_copy(at, half, parity):
        block = block_part(at, core, 2 * parity + half)
        to = r_peer(1 if half == 0 else 3)
        return remote(block, block, wy_send.at[at, half], wy_recv.at[at, half], to)

    def sib_copy(at, which, part):
        block = block_part(at, which, part)
        return remote(block, block, sib_send.at[at, part], sib_recv.at[at, part], (partner, me))

    def o_copy(s, slot):
        return remote(og_ref, ox.at[slot], o_send.at[s], o_recv.at[s], a_peer(s))

    def o_relay(half, slot):
        block = ox.at[slot, pl.ds(half * HALF, HALF)]
        return remote(block, block, o_send.at[2 * half], o_recv.at[2 * half], a_peer(1 if half == 0 else 3))

    def turned_rows(s, half, count):
        to = lax.rem(a + s, SIDE)
        return turned.at[pl.ds(pl.multiple_of(to * MODEL + half * (MODEL // 2), HALF), count)]

    def g_copy(s, slot):
        return remote(turned_rows(s, 0, MODEL), gx.at[slot], g_send.at[s], g_recv.at[s], a_peer(s))

    def g_far(half):
        to = a_peer(1 if half == 0 else 3)
        return remote(turned_rows(2, half, MODEL // 2), relay.at[half], r_send.at[half], r_recv.at[half], to)

    def g_relay(half, slot):
        block = gx.at[slot, pl.ds(half * (MODEL // 2), MODEL // 2)]
        return remote(relay.at[half], block, g_send.at[2 * half], g_recv.at[2 * half], a_peer(1 if half == 0 else 3))

    def y_far(half):
        block = partial.at[2, pl.ds(half * (OWN // 2), OWN // 2)]
        return remote(block, ybuf.at[half], yf_send.at[half], yf_recv.at[half], r_peer(1 if half == 0 else 3))

    def y_near(side, half):
        rows = pl.ds(half * (OWN // 2), OWN // 2)
        s, slot = 1 + 2 * side, 2 * side + half
        return remote(partial.at[s, rows], landing.at[side, rows], y_send.at[slot], y_recv.at[slot], r_peer(s))

    def square_copy(to, slot):
        return remote(square_own, squares.at[slot], q_send.at[to], q_recv.at[slot], (dp, to))

    pair_copy = remote(chunks.at[1 - core], paired, pair_send, pair_recv, (partner, me))

    def z_copy(to, slot):
        return remote(zsend.at[to], zrecv.at[slot], z_send.at[to], z_recv.at[slot], (2 * to + core, me))

    def piece(ref, owner):
        row = pl.multiple_of(lax.div(owner, SIDE) * THIN, THIN)
        return ref.at[pl.ds(row, THIN), lane_block(lax.rem(owner, SIDE), MODEL)]

    def fac_copy(to, slot):
        return remote(fac, facs.at[slot], f_send.at[to], f_recv.at[slot], (dp, to))

    def push_copy(src, to, slot):
        return remote(piece(pushed, src), arrived.at[slot], p_send.at[to], p_recv.at[slot], (dp, to))

    def back_copy(to, owner):
        return remote(back.at[to], piece(landed, owner), b_send.at[to], b_recv.at[owner], (dp, to))


    for at in range(GROUPS):
        steps[at, :GROUP, :] = st_ref[at * GROUP : (at + 1) * GROUP, :]
    rate_rows = jnp.broadcast_to(jnp.exp(lr_ref[...]), (HALF, HEADS)).T
    for at in range(GROUPS):
        rates[at, :GROUP, :] = rate_rows[at * GROUP : (at + 1) * GROUP, :]
    square = (TOK, TOK)
    coup[...] = jnp.where(rows_of(square) >= lanes_of(square), dot_nt(c_ref[...], b_ref[...]), 0.0)
    upper[...] = jnp.where(rows_of(square) <= lanes_of(square), 1.0, 0.0).astype(F32)
    ct[...] = c_ref[...].astype(F32).T.astype(BF16)
    acc[...] = jnp.zeros_like(acc)
    fac[...] = jnp.zeros_like(fac)

    def forward(at, carry):
        slot = lax.rem(at, 2)

        @pl.when(at + 1 < GROUPS)
        def _():
            for copy in load_group(at + 1):
                copy.start()

        step = steps[at, :GROUP, :]
        drop = -(rates[at, :GROUP, :1] * step)
        cumulative = jnp.dot(drop, upper[...], preferred_element_type=F32, precision=HIGHEST)
        shifted = cumulative - jnp.log(step)
        cums[at, :GROUP, :] = cumulative
        shifts[at, :GROUP, :] = shifted
        columns = cumulative.T
        fac[pl.ds(at, 1), :GROUP] = jnp.exp(columns[TOK - 1 :, :])
        for copy in load_group(at):
            copy.wait()
        load_gate(at).wait()
        for pair in range(GROUP // 2):
            here = slice(pair * HALF, (pair + 1) * HALF)
            parts = split_pair(xbuf[slot, :, here])
            top = bottom = None
            for which in range(2):
                head = 2 * pair + which
                col = columns[:, head : head + 1]
                row = shifted[head : head + 1, :]
                m_top = jnp.exp(jnp.minimum(col[:HALF] - row[:, :HALF], CAP)) * coup[:HALF, :HALF]
                m_bot = jnp.exp(jnp.minimum(col[HALF:] - row, CAP)) * coup[HALF:, :]
                t = dot(m_top.astype(BF16), parts[which][:HALF])
                b = dot(m_bot.astype(BF16), parts[which])
                top = t if top is None else top + t
                bottom = b if bottom is None else bottom + b
            inside = jnp.concatenate([top, bottom], axis=0)
            carried = dot_nt(c_ref[...], sbuf[slot, here, :])
            value = inside + carried * jnp.exp(pair_cols(columns, pair))
            lanes = pl.ds(pl.multiple_of(at * LANES + pair * HALF, HALF), HALF)
            mix = value * silu(z_ref[:, lanes].astype(F32))
            mixed[at, :, here] = mix
            acc[...] += mix * mix
        return carry

    def arriving(turn, half):
        for way in (0, 1):
            if turn < 3 or half == way:
                yield way, lax.rem(z + (RING - turn - 1 if way == 0 else turn + 1), RING)

    def arrive(turn, half):
        for way, at in arriving(turn, half):
            ring_copy(way, turn, half, at).wait_recv()
            if turn < 2 or (turn == 2 and half == way):
                ring_copy(way, turn + 1, half, at).start()
            side_copy(at, half, odd).start()
            sib_copy(at, core, 2 * odd + half).start()

    def arrive_side(turn, half):
        for _, at in arriving(turn, half):
            side_copy(at, half, 1 - odd).wait_recv()
            sib_copy(at, core, 2 * (1 - odd) + half).start()

    lax.fori_loop(0, EARLY, forward, 0)
    pl.semaphore_wait(barrier, CTX - 1 + RING - 1 + 1)
    def push_to(to):
        @pl.when(to != me)
        def _():
            push_copy(to, to, me).start()

    each_thin_out(lambda i: thin_send(i).start())
    lax.fori_loop(EARLY, THINAT, forward, 0)

    def wait_thin(i, carry):
        k = RING * odd + i

        @pl.when(k != me)
        def _():
            thin_from(i).wait_recv()

        return carry

    @pl.when(part_of == odd)
    def _():
        thin[lax.rem(me, RING)] = wpad[...]

    lax.fori_loop(0, RING, wait_thin, 0)
    rows = []
    for k in range(RING):
        value = thin[k].astype(F32)
        rest = [value[4 * i : 4 * i + 4, MODEL:] for i in range(SIDE)]
        rows += [value[:, :MODEL], jnp.concatenate(rest, axis=1)[:, :MODEL]]
    half_rows = pl.ds(pl.multiple_of(core * OWN + odd * (OWN // 2), 16), OWN // 2)
    full[z, half_rows] = jnp.concatenate(rows, axis=0).astype(BF16)
    for half in range(2):
        for way in range(2):
            ring_copy(way, 0, half, z).start()
        side_copy(z, half, odd).start()
        sib_copy(z, core, 2 * odd + half).start()
    for s in (1, 3):
        o_copy(s, a).start()
    lax.fori_loop(THINAT, GROUPS, forward, 0)

    inverse = lax.rsqrt(jnp.sum(acc[...], axis=1, keepdims=True) * (1.0 / INNER) + NORM_EPS)
    rms[...] = jnp.broadcast_to(inverse, rms.shape)

    def finish_norm(at, carry):
        lanes = lane_block(at, LANES)
        normed = mixed[at] * rms[:, :1] * gain_ref[:, lanes]
        gated[at] = normed.astype(BF16)
        rows = normed.T.astype(BF16)
        for which in range(2):
            block = 2 * at + which
            place = jnp.where(first, block, SIDE * lax.rem(block, SIDE) + lax.div(block, SIDE))
            turned[pl.ds(pl.multiple_of(place * OWN, OWN), OWN), :] = rows[which * OWN : (which + 1) * OWN]
        return carry

    lax.fori_loop(0, GROUPS, finish_norm, 0)

    for half in range(2):
        g_far(half).start()
    for s in (1, 3):
        g_copy(s, a).start()

    left, right = lax.rem(a + 3, SIDE), lax.rem(a + 1, SIDE)
    gx[a] = turned[pl.ds(pl.multiple_of(a * MODEL, MODEL), MODEL), :]
    ox[a] = og_ref[...]
    others(lambda to: fac_copy(to, me).start())
    acc[...] = jnp.zeros_like(acc)

    def product(at):
        for part in range(SIDE):
            sib_copy(at, 1 - core, part).wait_recv()
        value = dot_nt(og_ref[...], full[at])
        mixed[at] = value
        both = value * gated[at].astype(F32)
        total = acc[...]
        for i in range(LANES // HALF):
            total += both[:, i * HALF : (i + 1) * HALF]
        acc[...] = total

    def weight_part(s):
        rows = pl.ds(pl.multiple_of(lax.rem(r + s, SIDE) * OWN, OWN), OWN)
        total = None
        for source in range(SIDE):
            part = dot(gx[source, rows, :], ox[source])
            total = part if total is None else total + part
        partial[s] = total.astype(BF16)

    def near(step):
        return lax.rem(z + step, RING)

    arrive(0, 0)
    arrive(0, 1)
    o_copy(1, left).wait_recv()
    o_relay(0, left).start()
    o_copy(3, right).wait_recv()
    o_relay(1, right).start()
    for half in range(2):
        side_copy(z, half, 1 - odd).wait_recv()
        sib_copy(z, core, 2 * (1 - odd) + half).start()
    arrive(1, 0)
    arrive_side(0, 0)
    product(z)
    arrive(1, 1)
    arrive_side(0, 1)
    for half in range(2):
        g_far(half).wait_recv()
        g_relay(half, left if half == 0 else right).start()
    arrive(2, 0)
    arrive_side(1, 0)
    product(near(1))
    product(near(7))
    arrive(2, 1)
    arrive_side(1, 1)
    arrive(3, 0)
    arrive_side(2, 0)
    product(near(2))
    product(near(6))
    arrive(3, 1)
    arrive_side(2, 1)
    arrive_side(3, 0)
    product(near(3))
    product(near(5))
    arrive_side(3, 1)
    far = lax.rem(a + 2, SIDE)
    for half in range(2):
        o_relay(half, far).wait_recv()
        g_relay(half, far).wait_recv()
    g_copy(1, left).wait_recv()
    g_copy(3, right).wait_recv()
    weight_part(2)
    for half in range(2):
        y_far(half).start()
    weight_part(1)
    y_near(0, 1).start()
    weight_part(3)
    y_near(1, 0).start()
    product(near(4))
    weight_part(0)
    for half in range(2):
        y_far(half).wait_recv()
        at = slice(half * (OWN // 2), (half + 1) * (OWN // 2))
        added = partial[1 + 2 * half, at].astype(F32) + ybuf[half].astype(F32)
        partial[1 + 2 * half, at] = added.astype(BF16)
        y_near(half, half).start()
    mean = jnp.sum(acc[...], axis=1, keepdims=True) * (1.0 / INNER)
    acc[...] = jnp.broadcast_to(mean, acc.shape)

    def norm_back(at, carry):
        columns = cums[at].T
        for pair in range(GROUP // 2):
            here = slice(pair * HALF, (pair + 1) * HALF)
            lanes = pl.ds(pl.multiple_of(at * LANES + pair * HALF, HALF), HALF)
            gain = gain_ref[:, lanes]
            inner = gain * mixed[at, :, here] - gated[at, :, here].astype(F32) * (1.0 / gain) * acc[...]
            yg = silu(z_ref[:, lanes].astype(F32)) * rms[...] * inner
            gated[at, :, here] = yg.astype(BF16)
            weighted = (yg * jnp.exp(pair_cols(columns, pair))).astype(BF16)
            pushed[:, lanes] = dot(ct[...], weighted).astype(BF16)
        return carry

    for shift in (2, 1, 3, 0):
        quarter = lax.rem(y + shift, SIDE)
        lax.fori_loop(2 * quarter, 2 * quarter + 2, norm_back, 0)
        for row in range(SIDE):
            push_to(SIDE * lax.rem(x + (2, 1, 3, 0)[row], SIDE) + quarter)

    coup[...] = jnp.where(rows_of(square) <= lanes_of(square), dot_nt(b_ref[...], c_ref[...]), 0.0)

    def inside_back(at, carry):
        shifted = shifts[at]
        columns = shifted.T
        for pair in range(GROUP // 2):
            here = slice(pair * HALF, (pair + 1) * HALF)
            parts = split_pair(gated[at, :, here])
            top = bottom = None
            for which in range(2):
                head = 2 * pair + which
                col = columns[:, head : head + 1]
                row = cums[at, head : head + 1, :]
                m_top = jnp.exp(jnp.minimum(row - col[:HALF], CAP)) * coup[:HALF, :]
                m_bot = jnp.exp(jnp.minimum(row[:, HALF:] - col[HALF:], CAP)) * coup[HALF:, HALF:]
                t = dot(m_top.astype(BF16), parts[which])
                b = dot(m_bot.astype(BF16), parts[which][HALF:])
                top = t if top is None else top + t
                bottom = b if bottom is None else bottom + b
            mixed[at, :HALF, here] = top
            mixed[at, HALF:, here] = bottom
        return carry

    lax.fori_loop(0, 4, inside_back, 0)
    lax.fori_loop(4, GROUPS, inside_back, 0)
    for side in range(2):
        for half in range(2):
            y_near(side, half).wait_recv()
    total = partial[0].astype(F32)
    for side in range(2):
        total += landing[side].astype(F32)
    term[:OWN, :] = total
    term[OWN:, :] = jnp.zeros((WIDE - OWN, MODEL), F32)
    folded = jnp.sum((total * total).reshape(OWN // 8, 8, MODEL), axis=0)
    part = folded[:, :HALF]
    for i in range(1, MODEL // HALF):
        part += folded[:, i * HALF : (i + 1) * HALF]
    square_own[...] = part
    others(lambda to: square_copy(to, me).start())

    arrived[me] = piece(pushed, me)[...]
    facs[me] = fac[...]
    others(lambda k: fac_copy(k, k).wait_recv())
    shape = (HALF, LANES)
    hot = jnp.where(rows_of(shape) == lax.shift_right_logical(lanes_of(shape), 6), 1.0, 0.0).astype(F32)
    listed = jnp.concatenate([facs[k] for k in range(CTX)], axis=0)
    expanded[...] = jnp.dot(listed, hot, preferred_element_type=F32, precision=HIGHEST)
    running[...] = jnp.zeros_like(running)

    def chain(turn, carry):
        k = CTX - 1 - turn

        @pl.when(k != me)
        def _():
            push_copy(k, k, k).wait_recv()

        now = running[...]
        back[k] = now.astype(BF16)

        first = k * GROUPS + 2 * lax.rem(me, SIDE)
        factor = jnp.concatenate([expanded[pl.ds(first, 1), :], expanded[pl.ds(first + 1, 1), :]], axis=1)
        running[...] = factor * now + arrived[k].astype(F32)
        return carry

    lax.fori_loop(0, CTX, chain, 0)
    piece(landed, me)[...] = back[me]
    others(lambda to: back_copy(to, me).start())
    others(lambda k: square_copy(k, k).wait_recv())
    squares[me] = square_own[...]
    all_squares = squares[0]
    for k in range(1, CTX):
        all_squares += squares[k]
    whole = jnp.sum(jnp.sum(all_squares, axis=1, keepdims=True), axis=0, keepdims=True)
    clip = jnp.minimum(1.0, lax.rsqrt(whole + CLIP_EPS)) * scale
    for i in range(MODEL // HALF):
        block = (term[:, i * HALF : (i + 1) * HALF] * clip).T
        lo = i * HALF
        while lo < (i + 1) * HALF:
            owner = lo // COLS
            hi = min((i + 1) * HALF, (owner + 1) * COLS)
            at = slice(lo - owner * COLS, hi - owner * COLS)
            chunks[owner % 2, owner // 2, at] = block[lo - i * HALF : hi - i * HALF].astype(BF16)
            lo = hi
    pair_copy.start()

    def combine(at, count):
        slot = count % 2
        if count >= 2:
            store_group(at, slot).wait()
        last = (cums[at][:, TOK - 1 :] - shifts[at]).T
        ended = dot(b_ref[...], landed[:, lane_block(at, LANES)])
        for pair in range(GROUP // 2):
            here = slice(pair * HALF, (pair + 1) * HALF)
            value = mixed[at, :, here] + ended[:, here] * jnp.exp(pair_cols(last, pair))
            xbuf[slot, :, here] = value.astype(BF16)
        store_group(at, slot).start()

    pair_copy.wait_recv()

    def add_pair(i, carry):
        zsend[i] = (chunks[core, i].astype(F32) + paired[i].astype(F32)).astype(BF16)
        return carry

    lax.fori_loop(0, RING, add_pair, 0)
    z_others(lambda to: z_copy(to, z).start())
    for turn, shift in enumerate((0, 1, 3, 2)):
        quarter = lax.rem(y + shift, SIDE)

        def wait_back(row, carry):
            k = SIDE * row + quarter

            @pl.when(k != me)
            def _():
                back_copy(me, k).wait_recv()

            return carry

        lax.fori_loop(0, SIDE, wait_back, 0)
        for i in range(2):
            combine(2 * quarter + i, 2 * turn + i)
    z_others(lambda k: z_copy(k, k).wait_recv())
    zrecv[z] = zsend[z]
    summed = zrecv[0].astype(F32)
    for k in range(1, RING):
        summed += zrecv[k].astype(F32)
    grad_ref[...] = summed[:, :OWN]

    store_group(0, 0).wait()
    store_group(0, 1).wait()

    def finish(to):
        fac_copy(to, me).wait_send()
        push_copy(to, to, me).wait_send()
        square_copy(to, me).wait_send()
        back_copy(to, me).wait_send()

    others(finish)
    pair_copy.wait_send()
    z_others(lambda to: z_copy(to, z).wait_send())
    each_thin_out(lambda i: thin_send(i).wait_send())
    for s in (1, 3):
        o_copy(s, a).wait_send()
        g_copy(s, a).wait_send()
    for half in range(2):
        o_relay(half, left if half == 0 else right).wait_send()
        g_far(half).wait_send()
        g_relay(half, left if half == 0 else right).wait_send()
        y_far(half).wait_send()
        for side in range(2):
            y_near(side, half).wait_send()
    for turn in range(4):
        for half in range(2):
            for way in range(2):
                if turn == 3 and half != way:
                    continue
                at = lax.rem(z + (RING - turn if way == 0 else turn), RING)
                ring_copy(way, turn, half, at).wait_send()

    def finish_sib(at, carry):
        for part in range(SIDE):
            sib_copy(at, core, part).wait_send()
        return carry

    lax.fori_loop(0, RING, finish_sib, 0)

    def finish_side(at):
        for half in range(2):
            side_copy(at, half, odd).wait_send()

    z_others(finish_side)
    finish_side(z)


def layer(scale, *operands):
    vmem = pl.BlockSpec(memory_space=pltpu.VMEM)
    hbm = pl.BlockSpec(memory_space=pl.ANY)
    dma = pltpu.SemaphoreType.DMA
    ram = pltpu.VMEM
    return pl.pallas_call(
        functools.partial(layer_kernel, scale),
        out_shape=(jax.ShapeDtypeStruct((TOK, INNER), BF16), jax.ShapeDtypeStruct((COLS, OWN), F32)),
        in_specs=[hbm, hbm, vmem, vmem, hbm] + [vmem] * 5,
        out_specs=(hbm, vmem),
        scratch_shapes=[
            ram((GROUPS, 16, TOK), F32),
            ram((GROUPS, 16, HALF), F32),
            ram((GROUPS, 16, TOK), F32),
            ram((GROUPS, 16, TOK), F32),
            ram((2, TOK, LANES), BF16),
            ram((2, LANES, STATE), BF16),
            ram((TOK, INNER), BF16),
            ram((GROUPS, TOK, LANES), F32),
            ram((GROUPS, TOK, LANES), BF16),
            ram((TOK, TOK), F32),
            ram((TOK, TOK), F32),
            ram((TOK, HALF), F32),
            ram((TOK, HALF), F32),
            ram((INNER, TOK), BF16),
            ram((16, MODEL + WIDE), BF16),
            ram((RING, 16, MODEL + WIDE), BF16),
            ram((RING, 2 * OWN, MODEL), BF16),
            ram((SIDE, MODEL, TOK), BF16),
            ram((SIDE, TOK, MODEL), BF16),
            ram((SIDE, OWN, MODEL), BF16),
            ram((2, OWN, MODEL), BF16),
            ram((2, MODEL // 2, TOK), BF16),
            ram((2, OWN // 2, MODEL), BF16),
            ram((WIDE, MODEL), F32),
            ram((8, HALF), F32),
            ram((CTX, 8, HALF), F32),
            ram((2, RING, COLS, WIDE), BF16),
            ram((RING, COLS, WIDE), BF16),
            ram((RING, COLS, WIDE), BF16),
            ram((RING, COLS, WIDE), BF16),
            ram((8, HALF), F32),
            ram((CTX, 8, HALF), F32),
            ram((HALF, LANES), F32),
            ram((STATE, TOK), BF16),
            ram((STATE, INNER), BF16),
            ram((CTX, THIN, MODEL), BF16),
            ram((THIN, MODEL), F32),
            ram((CTX, THIN, MODEL), BF16),
            ram((STATE, INNER), BF16),
        ]
        + [dma((GROUPS,))]
        + [dma((2,))] * 3
        + [dma((RING,))] * 2
        + [dma((16,))] * 2
        + [dma((RING, 2))] * 2
        + [dma((RING, SIDE))] * 2
        + [dma((SIDE,))] * 6
        + [dma((2,))] * 4
        + [dma((CTX,))] * 2
        + [dma, dma]
        + [dma((RING,))] * 2
        + [dma((CTX,))] * 6,
        compiler_params=pltpu.CompilerParams(
            collective_id=0, has_side_effects=True, vmem_limit_bytes=VMEM_BYTES
        ),
        cost_estimate=pl.CostEstimate(flops=14 * 10**9, bytes_accessed=100 * 10**6, transcendentals=3 * 10**7),
        name="layer",
    )(*operands)


def per_device(
    ssm_input,
    gate_input,
    input_map,
    output_map,
    step_size,
    log_rate,
    entry_state,
    norm_gain,
    out_weight,
    out_grad,
):
    scale = math.sqrt(INNER * MODEL / lax.axis_size("dp"))
    input_grad, summed = layer(
        scale,
        ssm_input[0],
        gate_input[0],
        step_size[0],
        log_rate.reshape(1, HEADS),
        entry_state.reshape(INNER, STATE),
        input_map[0],
        output_map[0],
        norm_gain.reshape(1, INNER),
        out_weight,
        out_grad[0],
    )
    return (input_grad[None], summed.T)


def solution(mesh):
    placed = (
        P("dp", "ctx", None),
        P("dp", "ctx", None),
        P("dp", "ctx", None),
        P("dp", "ctx", None),
        P("dp", None, "ctx"),
        P(),
        P("dp", "ctx", None, None, None),
        P(),
        P(("dp", "ctx"), None),
        P("dp", "ctx", None),
    )
    return jax.shard_map(
        per_device,
        mesh=mesh,
        in_specs=placed,
        out_specs=(P("dp", "ctx", None), P("ctx", "dp")),
        check_vma=False,
    )
```
